128 devices in a mesh: gy: 8 (over y_hi, x), gz: 16 (over y_lo, z, core).
Axes of the slice: x: 4, y: 4 (y_hi: 2, y_lo: 2; y = y_hi * 2 + y_lo), z: 4, core: 2. Of those that a mesh axis runs over, the one named last changes fastest.
Arguments:
- kspace: bfloat16 [2, 16, 64, 512, 128], P(None, None, 'gz', 'gy'), may hold values from -6 to 6
- measured: bfloat16 [2, 16, 64, 512, 128], P(None, None, 'gz', 'gy'), may hold values from -6 to 6
- sample_mask: int32 [64, 512], P('gz', 'gy'), may hold values 0 or 1
- step_size: float32 [1], replicated, may hold values from 0.3 to 1
- coil_field: bfloat16 [2, 128, 16, 64, 512], P(None, ('gy', 'gz')), may hold values from -1 to 1
- conv_in: bfloat16 [32, 2, 3, 3, 3], replicated, may hold values from -0.875 to 0.875
- bias_in: float32 [32], replicated, may hold values from -3 to 3
- conv_out: bfloat16 [2, 32, 3, 3, 3], replicated, may hold values from -0.5 to 0.5
- cotangent: bfloat16 [2, 16, 64, 512, 128], P(None, None, 'gz', 'gy'), may hold values from -6 to 6
Outputs:
- kspace_next: bfloat16 [2, 16, 64, 512, 128], P(None, None, 'gz', 'gy')
- grad_conv_in: float32 [32, 2, 3, 3, 3], replicated
- grad_bias_in: float32 [32], replicated
- grad_conv_out: float32 [2, 32, 3, 3, 3], replicated
The draws below stay inside these ranges and needn't reach their ends.
All inputs are finite; a program needn't handle non-finite values. No bound on the sum of `sample_mask` on one device may be relied on, other than what follows from the above.
Results may differ from the reference program's by a relative error of at most 0.012.
Values may be sent and summed in bfloat16 or wider, within the bound.
A program may use at most 256 MiB of HBM per device.

```python
import math
import jax
import jax.numpy as jnp
from jax import lax

C = 16
Y = 512
Z = 64
F = 32
X = 128


def place_ends(drawn, own_key, low, top_value):
    longest = drawn.shape.index(max(drawn.shape))
    spots = []
    for shift in (0, 1):
        where = [jax.random.randint(jax.random.fold_in(own_key, axis), (), 0, length) for axis, length in enumerate(drawn.shape)]
        where[longest] = (where[longest] + shift) % drawn.shape[longest]
        spots.append(tuple(where))
    return drawn.at[spots[0]].set(low).at[spots[1]].set(top_value)


def steps_of(own_key, extent, cuts, least, largest):
    def one(position, shards_of):
        steps = jax.random.uniform(jax.random.fold_in(jax.random.fold_in(own_key, 6), position), (shards_of,), jnp.float32, least / len(cuts), largest / len(cuts))
        return jnp.repeat(jnp.exp(steps), extent[position] // shards_of).reshape((-1,) + (1,) * (len(extent) - position - 1))

    factor_of = one(*cuts[0])
    for cut in cuts[1:]:
        factor_of = factor_of * one(*cut)
    return factor_of


def centred(key, dims, scale, limit, split=(), kind=jnp.bfloat16):
    drawn = jax.random.normal(key, dims, jnp.float32) * scale
    if len(split) > 0:
        drawn = steps_of(key, dims, split, -0.22, 0.18) * drawn
    return jnp.clip(drawn, min=-limit, max=limit).astype(kind)


def setup_inputs(seed: int = 0) -> dict:
    key_list = jax.random.split(jax.random.key(seed), 10)
    kspace = centred(key_list[0], (2, C, Z, Y, X), 1.0, 6.0, ((2, 16), (3, 8)))
    measured = centred(key_list[1], (2, C, Z, Y, X), 1.0, 6.0, ((2, 16), (3, 8)))
    sample_mask = place_ends((jax.random.randint(key_list[2], (Z, Y), 0, 3) < 1).astype(jnp.int32), jax.random.fold_in(key_list[2], 1), 0, 1)
    step_size = jnp.clip(jax.random.uniform(key_list[3], (1,), jnp.float32, 0.3, 1.0), 0.3, 1.0)
    coil_field = centred(key_list[4], (2, X, C, Z, Y), 0.18, 1.0, ((1, 128),))
    conv_in = centred(key_list[5], (F, 2, 3, 3, 3), 54 ** -0.5, 0.875)
    bias_in = centred(key_list[6], (F,), 0.5, 3.0, (), jnp.float32)
    conv_out = centred(key_list[7], (2, F, 3, 3, 3), (4 * F) ** -0.5, 0.5)
    cotangent = centred(key_list[8], (2, C, Z, Y, X), 1.0, 6.0, ((2, 16), (3, 8)))
    return dict(kspace=kspace, measured=measured, sample_mask=sample_mask, step_size=step_size, coil_field=coil_field, conv_in=conv_in, bias_in=bias_in, conv_out=conv_out, cotangent=cotangent)


def dft_tables(length):
    index_range = jnp.arange(length, dtype=jnp.int32)
    phase_index = index_range[:, None] * index_range[None, :] % length
    angle_table = phase_index.astype(jnp.float32) * (2.0 * math.pi / length)
    factor = 1.0 / math.sqrt(length)
    return ((jnp.cos(angle_table) * factor).astype(jnp.bfloat16), (jnp.sin(angle_table) * factor).astype(jnp.bfloat16))

def transform(spectrum, formula, tables, inverse):
    values = spectrum.astype(jnp.float32)
    cosine = jnp.einsum(formula, values, tables[0].astype(jnp.float32), precision=lax.Precision.HIGHEST)
    sine_part = jnp.einsum(formula, values, tables[1].astype(jnp.float32), precision=lax.Precision.HIGHEST)
    if inverse:
        real_part = cosine[0] - sine_part[1]
        imag_part = cosine[1] + sine_part[0]
    else:
        real_part = cosine[0] + sine_part[1]
        imag_part = cosine[1] - sine_part[0]
    return jnp.stack([real_part, imag_part])

def to_image(spectrum, sens_field, tables_y, tables_z):
    hybrid = transform(spectrum, 'pczyx,yY->pczYx', tables_y, True).astype(jnp.bfloat16)
    coil_images = transform(hybrid, 'pczyx,zZ->pcZyx', tables_z, True)
    sens_real = sens_field[0].astype(jnp.float32)
    sens_imag = sens_field[1].astype(jnp.float32)
    real_part = lax.optimization_barrier(jnp.sum(sens_real * coil_images[0] + sens_imag * coil_images[1], axis=0))
    imag_part = lax.optimization_barrier(jnp.sum(sens_real * coil_images[1] - sens_imag * coil_images[0], axis=0))
    return jnp.stack([real_part, imag_part]).astype(jnp.bfloat16)

def conv_three(volume, kernel):
    return lax.conv_general_dilated(volume[None], kernel, (1, 1, 1), 'SAME', dimension_numbers=('NCDHW', 'OIDHW', 'NCDHW'), precision=lax.Precision.HIGHEST)[0]

def reference(kspace, measured, sample_mask, step_size, coil_field, conv_in, bias_in, conv_out, cotangent):
    tables_y = dft_tables(Y)
    tables_z = dft_tables(Z)
    sens_field = jnp.transpose(coil_field, (0, 2, 3, 4, 1))
    image_field = to_image(kspace, sens_field, tables_y, tables_z)
    kernel_in = conv_in.astype(jnp.float32)
    kernel_out = conv_out.astype(jnp.float32)
    pre_act = conv_three(image_field.astype(jnp.float32), kernel_in) + bias_in[:, None, None, None]
    hidden = jax.nn.silu(pre_act).astype(jnp.bfloat16)
    refine_image = conv_three(hidden.astype(jnp.float32), kernel_out).astype(jnp.bfloat16)
    sens_real = sens_field[0].astype(jnp.float32)
    sens_imag = sens_field[1].astype(jnp.float32)
    refine_real = refine_image[0].astype(jnp.float32)[None]
    refine_imag = refine_image[1].astype(jnp.float32)[None]
    coil_refine = jnp.stack([sens_real * refine_real - sens_imag * refine_imag, sens_real * refine_imag + sens_imag * refine_real]).astype(jnp.bfloat16)
    partial_z = transform(coil_refine, 'pczyx,zZ->pcZyx', tables_z, False).astype(jnp.bfloat16)
    refine = transform(partial_z, 'pczyx,yY->pczYx', tables_y, False).astype(jnp.bfloat16)
    weight = sample_mask.astype(jnp.float32)[None, None, :, :, None]
    current = kspace.astype(jnp.float32)
    kspace_next = (current - step_size[0] * weight * (current - measured.astype(jnp.float32)) + refine.astype(jnp.float32)).astype(jnp.bfloat16)
    grad_image = to_image(cotangent, sens_field, tables_y, tables_z)
    unused_out, pull_out = jax.vjp(conv_three, hidden.astype(jnp.float32), kernel_out)
    back_hidden, grad_out = pull_out(grad_image.astype(jnp.float32))
    sigmoid_pre = jax.nn.sigmoid(pre_act)
    back_pre = (back_hidden * sigmoid_pre * (1.0 + pre_act * (1.0 - sigmoid_pre))).astype(jnp.bfloat16)
    unused_in, pull_in = jax.vjp(conv_three, image_field.astype(jnp.float32), kernel_in)
    unused_image, grad_in = pull_in(back_pre.astype(jnp.float32))
    grad_bias = lax.optimization_barrier(jnp.sum(back_pre.astype(jnp.float32), axis=(1, 2, 3)))
    norm_factor = 1.0 / math.sqrt(X * Y * Z)
    return (kspace_next, grad_in * norm_factor, grad_bias * norm_factor, grad_out * norm_factor)
```

```python
import math

import jax
import jax.numpy as jnp
import numpy as np
from jax import lax
from jax.experimental import pallas as pl
from jax.experimental.pallas import tpu as pltpu
from jax.sharding import PartitionSpec as P

MESH = pl.DeviceIdType.MESH
AXES = ("gy", "gz")
BF = jnp.bfloat16
F32 = jnp.float32
VMEM_LIMIT = 56 * 2**20
VM = pl.BlockSpec(memory_space=pltpu.VMEM)


def trig(length):
    index = np.arange(length, dtype=np.int64)
    angle = (index[:, None] * index[None, :] % length).astype(np.float64) * (2.0 * math.pi / length)
    factor = 1.0 / math.sqrt(length)
    return np.cos(angle) * factor, np.sin(angle) * factor


def as_bf16(array):
    return np.asarray(array, dtype=np.float32).astype(jnp.bfloat16)


def inverse_y_table(gy, rows):
    length = gy * rows
    cos, sin = trig(length)
    cos, sin = cos.reshape(gy, rows, length), sin.reshape(gy, rows, length)
    table = np.stack([np.stack([cos, sin], 2), np.stack([-sin, cos], 2)], 1)
    return as_bf16(table.reshape(2 * length, 2 * length))


def forward_y_table(gy, rows):
    length = gy * rows
    cos, sin = trig(length)
    cos, sin = cos.reshape(length, gy, rows), sin.reshape(length, gy, rows)
    table = np.stack([np.stack([cos, -sin], 2), np.stack([sin, cos], 2)], 0)
    return as_bf16(table.reshape(2 * length, 2 * length))


def z_table(length, inverse):
    cos, sin = trig(length)
    if inverse:
        table = np.block([[cos, -sin], [sin, cos]])
    else:
        table = np.block([[cos, sin], [-sin, cos]])
    return as_bf16(table)


def band_masks():
    zo, dz, j, zi = np.ogrid[0:8, 0:3, 0:3, 0:8]
    return (8 * (j - 1) + zi == zo + dz - 1).astype(np.float32)


def band_spread():
    hit = band_masks()
    eye = np.eye(18, dtype=np.float32)
    spread = np.einsum("odjz,kl->odkjlz", hit, eye)
    return as_bf16(spread.reshape(8, 54, 432))


def band_keep():
    hit = band_masks()
    keep = np.broadcast_to(hit.transpose(1, 0, 2, 3)[:, :, :, None, :], (3, 8, 3, 18, 8))
    return np.ascontiguousarray(keep.reshape(3, 8, 432)).astype(np.float32)


def band_gather():
    eye = np.eye(18, dtype=np.float32)
    return np.ascontiguousarray(np.broadcast_to(eye[None, :, None, :], (3, 18, 8, 18)).reshape(432, 18))


def out_spread():
    q, dz, zo = np.ogrid[0:10, 0:3, 0:8]
    hit = (q == zo + dz).astype(np.float32)
    eye = np.eye(18, dtype=np.float32)
    return as_bf16(np.einsum("qdz,kl->qdklz", hit, eye).reshape(10, 54, 144))


def call(body, outs, scratch, name):
    return pl.pallas_call(
        body,
        out_shape=outs,
        scratch_shapes=scratch,
        compiler_params=pltpu.CompilerParams(vmem_limit_bytes=VMEM_LIMIT),
        name=name,
    )


def pack_body(k_ref, out_ref, stage):
    def block(index, carry):
        depth, coil = index // 16, index % 16
        both = jnp.concatenate([k_ref[0, coil, depth], k_ref[1, coil, depth]], axis=0)
        stage[pl.ds(index, 128, stride=64), :] = both.astype(F32).T
        return carry

    lax.fori_loop(0, 64, block, 0, unroll=2)

    def row(x, carry):
        out_ref[x] = stage[pl.ds(pl.multiple_of(x * 64, 64), 64), :].astype(BF)
        return carry

    lax.fori_loop(0, 128, row, 0, unroll=4)


def pack(kspace):
    return call(
        pack_body,
        jax.ShapeDtypeStruct((128, 64, 128), BF),
        [pltpu.VMEM((8192, 128), F32)],
        "pack",
    )(kspace)


def image_body(tiles, sens, table_y, table_z, out_ref, half):
    def rows(m, carry):
        left = jnp.concatenate(
            [tiles[pl.ds(gy * 16 + m * 4, 4)].reshape(256, 128) for gy in range(8)], axis=1
        )
        done = jnp.dot(left, table_y[...], preferred_element_type=F32)
        for lt in range(8):
            span = pl.ds(pl.multiple_of(lt * 1024 + m * 256, 256), 256)
            half[span, :] = done[:, lt * 128 : lt * 128 + 128]
        return carry

    lax.fori_loop(0, 4, rows, 0)

    def coil(c, carry):
        real, imag = carry
        lines = [half[pl.ds(lt * 1024 + c, 64, stride=16), :].astype(BF) for lt in range(8)]
        lines = [jnp.concatenate(lines[4 * p : 4 * p + 4], axis=1) for p in range(2)]
        lines = jnp.concatenate(lines, axis=0)
        coil_image = jnp.dot(table_z[...], lines, preferred_element_type=F32)
        c_r, c_i = coil_image[:64], coil_image[64:]
        s_r, s_i = sens[0, 0, c].astype(F32), sens[1, 0, c].astype(F32)
        return real + (s_r * c_r + s_i * c_i), imag + (s_r * c_i - s_i * c_r)

    zero = jnp.zeros((64, 512), F32)
    real, imag = lax.fori_loop(0, 16, coil, (zero, zero))
    out_ref[0] = real.astype(BF)
    out_ref[1] = imag.astype(BF)


def to_image(tiles, sens, table_y, table_z, name):
    return call(
        image_body,
        jax.ShapeDtypeStruct((2, 64, 512), BF),
        [pltpu.VMEM((8192, 128), F32)],
        name,
    )(tiles, sens, table_y, table_z)


def shifted(value, dy):
    if dy == 1:
        return value
    lane = lax.broadcasted_iota(jnp.int32, value.shape, value.ndim - 1)
    if dy == 0:
        return jnp.where(lane == 0, 0.0, pltpu.roll(value, 1, value.ndim - 1))
    return jnp.where(lane == 511, 0.0, pltpu.roll(value, 511, value.ndim - 1))


def fill_columns(images, cols):
    cols[pl.ds(0, 144), :] = jnp.zeros((144, 512), BF)
    cols[pl.ds(1296, 144), :] = jnp.zeros((144, 512), BF)
    for dx, image in enumerate(images):
        parts = [image[i].astype(F32) for i in range(2)]
        for dy in range(3):
            pair = jnp.stack([shifted(part, dy).reshape(8, 8, 512) for part in parts], axis=1)
            pair = pair.reshape(8, 16, 512).astype(BF)
            for zb in range(8):
                cols[pl.ds((zb + 1) * 144 + (dy * 3 + dx) * 16, 16), :] = pair[zb]


def forward_body(
    left, mid, right, w_in, bias, w_out, cols, hidden, slope, q_up, q_mid, q_down
):
    fill_columns((left, mid, right), cols)
    hidden[pl.ds(0, 32), :] = jnp.zeros((32, 512), BF)
    hidden[pl.ds(65 * 32, 32), :] = jnp.zeros((32, 512), BF)

    def block(zb, carry):
        window = cols[pl.ds(pl.multiple_of(zb * 144, 16), 432), :]
        pre = jnp.dot(w_in[...], window, preferred_element_type=F32) + bias[...]
        sig = jax.nn.sigmoid(pre)
        hidden[pl.ds(pl.multiple_of(zb * 256 + 32, 32), 256), :] = (pre * sig).astype(BF)
        slope[pl.ds(pl.multiple_of(zb * 256, 256), 256), :] = sig * (1.0 + pre * (1.0 - sig))
        return carry

    lax.fori_loop(0, 8, block, 0)

    def out(zb, carry):
        window = hidden[pl.ds(pl.multiple_of(zb * 256, 256), 320), :]
        terms = jnp.dot(w_out[...], window, preferred_element_type=F32).reshape(18, 8, 512)
        rows = pl.ds(pl.multiple_of(zb * 8, 8), 8)
        for dx, target in enumerate((q_up, q_mid, q_down)):
            for o in range(2):
                base = (dx * 2 + o) * 3
                total = shifted(terms[base], 0) + terms[base + 1] + shifted(terms[base + 2], 2)
                target[o, rows, :] = total
        return carry

    lax.fori_loop(0, 8, out, 0)


def conv_forward(left, mid, right, w_in, bias, w_out):
    part = jax.ShapeDtypeStruct((2, 64, 512), F32)
    return call(
        forward_body,
        (
            jax.ShapeDtypeStruct((1440, 512), BF),
            jax.ShapeDtypeStruct((66 * 32, 512), BF),
            jax.ShapeDtypeStruct((2048, 512), F32),
            part,
            part,
            part,
        ),
        [],
        "conv_forward",
    )(left, mid, right, w_in, bias, w_out)


def spread_body(q_from_left, q_mid, q_from_right, sens, table_z, table_y, out_ref, half):
    image = [
        (q_from_left[o].astype(F32) + q_mid[o] + q_from_right[o].astype(F32)).astype(BF).astype(F32)
        for o in range(2)
    ]
    r_r, r_i = image

    def coil(c, carry):
        s_r, s_i = sens[0, 0, c].astype(F32), sens[1, 0, c].astype(F32)
        lines = jnp.concatenate([s_r * r_r - s_i * r_i, s_r * r_i + s_i * r_r], axis=0).astype(BF)
        done = jnp.dot(table_z[...], lines, preferred_element_type=F32)
        for lt in range(8):
            p, lane = lt // 4, lt % 4 * 128
            half[pl.ds(lt * 1024 + c, 64, stride=16), :] = done[p * 64 : p * 64 + 64, lane : lane + 128]
        return carry

    lax.fori_loop(0, 16, coil, 0)

    def rows(m, carry):
        left = [half[pl.ds(pl.multiple_of(lt * 1024 + m * 256, 256), 256), :] for lt in range(8)]
        left = jnp.concatenate([part.astype(BF) for part in left], axis=1)
        done = jnp.dot(left, table_y[...], preferred_element_type=F32).astype(BF)
        for gy in range(8):
            out_ref[pl.ds(gy * 16 + m * 4, 4)] = done[:, gy * 128 : gy * 128 + 128].reshape(4, 64, 128)
        return carry

    lax.fori_loop(0, 4, rows, 0)


def to_coils(q_from_left, q_mid, q_from_right, sens, table_z, table_y):
    return call(
        spread_body,
        jax.ShapeDtypeStruct((128, 64, 128), BF),
        [pltpu.VMEM((8192, 128), F32)],
        "to_coils",
    )(q_from_left, q_mid, q_from_right, sens, table_z, table_y)


def unpack_body(tiles, kspace, measured, weight, out_ref, stage):
    def row(x, carry):
        stage[pl.ds(pl.multiple_of(x * 64, 64), 64), :] = tiles[x].astype(F32)
        return carry

    lax.fori_loop(0, 128, row, 0, unroll=4)

    def block(index, carry):
        depth, coil = index // 16, index % 16
        both = stage[pl.ds(index, 128, stride=64), :].T
        share = weight[depth]
        for part in range(2):
            current = kspace[part, coil, depth].astype(F32)
            other = measured[part, coil, depth].astype(F32)
            refine = both[part * 64 : part * 64 + 64]
            out_ref[part, coil, depth] = (current - share * (current - other) + refine).astype(BF)
        return carry

    lax.fori_loop(0, 64, block, 0, unroll=2)


def unpack(tiles, kspace, measured, weight):
    return call(
        unpack_body,
        jax.ShapeDtypeStruct((2, 16, 4, 64, 128), BF),
        [pltpu.VMEM((8192, 128), F32)],
        "unpack",
    )(tiles, kspace, measured, weight)


def gather_terms(total, keep, gather):
    pieces = []
    total = total.reshape(8, 32, 432)
    for dz in range(3):
        kept = total[0] * keep[dz, 0:1, :]
        for zo in range(1, 8):
            kept = kept + total[zo] * keep[dz, zo : zo + 1, :]
        pieces.append(
            jnp.dot(kept, gather[...], preferred_element_type=F32, precision=lax.Precision.HIGHEST)
        )
    return pieces


def backward_body(
    left, mid, right, cols, hidden, slope, w_back, keep, gather, out_ref, cols_g, sum_in, sum_out, sum_b
):
    fill_columns((left, mid, right), cols_g)
    sum_in[...] = jnp.zeros_like(sum_in)
    sum_out[...] = jnp.zeros_like(sum_out)
    sum_b[...] = jnp.zeros_like(sum_b)
    nt = (((1,), (1,)), ((), ()))

    def block(zb, carry):
        span = pl.ds(pl.multiple_of(zb * 144, 16), 432)
        window_g = cols_g[span, :]
        back = jnp.dot(w_back[...], window_g, preferred_element_type=F32)
        back = (back * slope[pl.ds(pl.multiple_of(zb * 256, 256), 256), :]).astype(BF)
        sum_in[...] += lax.dot_general(back, cols[span, :], nt, preferred_element_type=F32)
        held = hidden[pl.ds(pl.multiple_of(zb * 256 + 32, 32), 256), :]
        sum_out[...] += lax.dot_general(held, window_g, nt, preferred_element_type=F32)
        wide = back.astype(F32)
        sum_b[...] += wide[:, :128] + wide[:, 128:256] + wide[:, 256:384] + wide[:, 384:]
        return carry

    lax.fori_loop(0, 8, block, 0)
    bias_sum = jnp.sum(sum_b[...].reshape(8, 32, 128), axis=0)
    bias_sum = jnp.sum(bias_sum, axis=1, keepdims=True)
    pieces = gather_terms(sum_in[...], keep, gather) + gather_terms(sum_out[...], keep, gather)
    pieces.append(jnp.broadcast_to(bias_sum, (32, 20)))
    out_ref[...] = jnp.concatenate(pieces, axis=1)


def conv_backward(left, mid, right, cols, hidden, slope, w_back, keep, gather):
    return call(
        backward_body,
        jax.ShapeDtypeStruct((32, 128), F32),
        [
            pltpu.VMEM((1440, 512), BF),
            pltpu.VMEM((256, 432), F32),
            pltpu.VMEM((256, 432), F32),
            pltpu.VMEM((256, 128), F32),
        ],
        "conv_backward",
    )(left, mid, right, cols, hidden, slope, w_back, keep, gather)


def reduce_body(count_y, count_z, in_ref, out_ref, first, second, sems):
    my_y, my_z = lax.axis_index("gy"), lax.axis_index("gz")

    def exchange(value, buffer, count, mine, device, send, recv):
        buffer[mine] = value

        def start(step, carry):
            to = lax.rem(mine + step, count)
            pltpu.make_async_remote_copy(
                src_ref=buffer.at[mine],
                dst_ref=buffer.at[mine],
                send_sem=send,
                recv_sem=recv,
                device_id=device(to),
                device_id_type=MESH,
            ).start()
            return carry

        lax.fori_loop(1, count, start, 0)
        every = pltpu.make_async_remote_copy(
            src_ref=buffer.at[pl.ds(0, count - 1)],
            dst_ref=buffer.at[pl.ds(0, count - 1)],
            send_sem=send,
            recv_sem=recv,
            device_id=device(mine),
            device_id_type=MESH,
        )
        every.wait_send()
        every.wait_recv()
        total = buffer[0]
        for index in range(1, count):
            total = total + buffer[index]
        return total

    over_z = exchange(
        in_ref[...], first, count_z, my_z, lambda to: (my_y, to), sems.at[0], sems.at[1]
    )
    out_ref[...] = exchange(
        over_z, second, count_y, my_y, lambda to: (to, my_z), sems.at[2], sems.at[3]
    )


def all_reduce(value, count_y, count_z):
    def body(*refs):
        reduce_body(count_y, count_z, *refs)

    return pl.pallas_call(
        body,
        out_shape=jax.ShapeDtypeStruct((32, 128), F32),
        in_specs=[VM],
        out_specs=VM,
        scratch_shapes=[
            pltpu.VMEM((count_z, 32, 128), F32),
            pltpu.VMEM((count_y, 32, 128), F32),
            pltpu.SemaphoreType.DMA((4,)),
        ],
        compiler_params=pltpu.CompilerParams(has_side_effects=True),
        name="all_reduce",
    )(value)


def on_device(
    kspace, measured, sample_mask, step_size, coil_field, conv_in, bias_in, conv_out, cotangent
):
    count_y, count_z = lax.axis_size("gy"), lax.axis_size("gz")
    devices = count_y * count_z
    row_tile, x_cells, depth_tile = kspace.shape[3], kspace.shape[4], kspace.shape[2]
    inverse_y = jnp.asarray(inverse_y_table(count_y, row_tile))
    forward_y = jnp.asarray(forward_y_table(count_y, row_tile))
    inverse_z = jnp.asarray(z_table(count_z * depth_tile, True))
    forward_z = jnp.asarray(z_table(count_z * depth_tile, False))
    spread = jnp.asarray(band_spread())
    keep = jnp.asarray(band_keep())
    gather = jnp.asarray(band_gather())
    spread_out = jnp.asarray(out_spread())

    flat_in = conv_in.transpose(0, 2, 3, 4, 1).reshape(32, 54)
    w_in = jnp.einsum("ok,zkc->zoc", flat_in, spread).reshape(256, 432)
    flat_back = conv_out[:, :, ::-1, ::-1, ::-1].transpose(1, 2, 3, 4, 0).reshape(32, 54)
    w_back = jnp.einsum("ok,zkc->zoc", flat_back, spread).reshape(256, 432)
    flat_out = conv_out.transpose(1, 2, 4, 0, 3).reshape(32, 54)
    w_out = jnp.einsum("ik,qkr->rqi", flat_out, spread_out).reshape(144, 320)
    bias = jnp.tile(bias_in, 8)[:, None]
    weight = jnp.broadcast_to(
        (step_size[0] * sample_mask.astype(F32))[:, :, None], (depth_tile, row_tile, x_cells)
    )

    def exchange(blocks):
        return lax.all_to_all(blocks, AXES, split_axis=0, concat_axis=0, tiled=True)

    up = [(i, i + 1) for i in range(devices - 1)]
    down = [(i + 1, i) for i in range(devices - 1)]

    def neighbours(image):
        return lax.ppermute(image, AXES, up), lax.ppermute(image, AXES, down)

    k_tiles = exchange(pack(kspace))
    g_tiles = exchange(pack(cotangent))
    image = to_image(k_tiles, coil_field, inverse_y, inverse_z, "image_k")
    left, right = neighbours(image)
    cols, hidden, slope, q_up, q_mid, q_down = conv_forward(left, image, right, w_in, bias, w_out)
    from_left = lax.ppermute(q_up, AXES, up)
    from_right = lax.ppermute(q_down, AXES, down)
    blocks = to_coils(from_left, q_mid, from_right, coil_field, forward_z, forward_y)
    refine = exchange(blocks)
    grad = to_image(g_tiles, coil_field, inverse_y, inverse_z, "image_g")
    g_left, g_right = neighbours(grad)
    terms = conv_backward(g_left, grad, g_right, cols, hidden, slope, w_back, keep, gather)
    totals = all_reduce(terms, count_y, count_z)
    kspace_next = unpack(refine, kspace, measured, weight)

    norm = 1.0 / math.sqrt(x_cells * row_tile * count_y * depth_tile * count_z)
    totals = totals * norm
    grad_in = totals[:, :54].reshape(32, 3, 3, 3, 2).transpose(0, 4, 1, 2, 3)
    grad_out = totals[:, 54:108].reshape(32, 3, 3, 3, 2).transpose(4, 0, 1, 2, 3)
    grad_out = grad_out[:, :, ::-1, ::-1, ::-1]
    return kspace_next, grad_in, totals[:, 108], grad_out


def solution(mesh):
    tile = P(None, None, "gz", "gy", None)
    in_specs = (
        tile,
        tile,
        P("gz", "gy"),
        P(),
        P(None, AXES, None, None, None),
        P(),
        P(),
        P(),
        tile,
    )
    out_specs = (tile, P(), P(), P())
    return jax.shard_map(
        on_device, mesh=mesh, in_specs=in_specs, out_specs=out_specs, check_vma=False
    )
```

```python
import math

import jax
import jax.numpy as jnp
import numpy as np
from jax import lax
from jax.experimental import pallas as pl
from jax.experimental.pallas import tpu as pltpu
from jax.sharding import PartitionSpec as P

MESH = pl.DeviceIdType.MESH
AXES = ("gy", "gz")
BF = jnp.bfloat16
F32 = jnp.float32
VMEM_LIMIT = 56 * 2**20
VM = pl.BlockSpec(memory_space=pltpu.VMEM)


def trig(length):
    index = np.arange(length, dtype=np.int64)
    angle = (index[:, None] * index[None, :] % length).astype(np.float64) * (2.0 * math.pi / length)
    factor = 1.0 / math.sqrt(length)
    return np.cos(angle) * factor, np.sin(angle) * factor


def as_bf16(array):
    return np.asarray(array, dtype=np.float32).astype(jnp.bfloat16)


def inverse_y_table(gy, rows):
    length = gy * rows
    cos, sin = trig(length)
    cos, sin = cos.reshape(gy, rows, length), sin.reshape(gy, rows, length)
    table = np.stack([np.stack([cos, sin], 2), np.stack([-sin, cos], 2)], 1)
    return as_bf16(table.reshape(2 * length, 2 * length))


def forward_y_table(gy, rows):
    length = gy * rows
    cos, sin = trig(length)
    cos, sin = cos.reshape(length, gy, rows), sin.reshape(length, gy, rows)
    table = np.stack([np.stack([cos, -sin], 2), np.stack([sin, cos], 2)], 0)
    return as_bf16(table.reshape(2 * length, 2 * length))


def z_table(length, inverse):
    cos, sin = trig(length)
    if inverse:
        table = np.block([[cos, -sin], [sin, cos]])
    else:
        table = np.block([[cos, sin], [-sin, cos]])
    return as_bf16(table)


def band_masks():
    zo, dz, j, zi = np.ogrid[0:8, 0:3, 0:3, 0:8]
    return (8 * (j - 1) + zi == zo + dz - 1).astype(np.float32)


def band_spread():
    hit = band_masks()
    eye = np.eye(18, dtype=np.float32)
    spread = np.einsum("odjz,kl->odkjlz", hit, eye)
    return as_bf16(spread.reshape(8, 54, 432))


def band_keep():
    hit = band_masks()
    keep = np.broadcast_to(hit.transpose(1, 0, 2, 3)[:, :, :, None, :], (3, 8, 3, 18, 8))
    return np.ascontiguousarray(keep.reshape(3, 8, 432)).astype(np.float32)


def band_gather():
    eye = np.eye(18, dtype=np.float32)
    return np.ascontiguousarray(np.broadcast_to(eye[None, :, None, :], (3, 18, 8, 18)).reshape(432, 18))


def out_spread():
    q, dz, zo = np.ogrid[0:10, 0:3, 0:8]
    hit = (q == zo + dz).astype(np.float32)
    eye = np.eye(18, dtype=np.float32)
    return as_bf16(np.einsum("qdz,kl->qdklz", hit, eye).reshape(10, 54, 144))


BATCH_A = 40


def shifted(value, dy):
    if dy == 1:
        return value
    lane = lax.broadcasted_iota(jnp.int32, value.shape, value.ndim - 1)
    if dy == 0:
        return jnp.where(lane == 0, 0.0, pltpu.roll(value, 1, value.ndim - 1))
    return jnp.where(lane == 511, 0.0, pltpu.roll(value, 511, value.ndim - 1))


def fill_columns(images, cols):
    cols[pl.ds(0, 144), :] = jnp.zeros((144, 512), BF)
    cols[pl.ds(1296, 144), :] = jnp.zeros((144, 512), BF)
    for dx, image in enumerate(images):
        parts = [image(i) for i in range(2)]
        for dy in range(3):
            pair = jnp.stack([shifted(part, dy).reshape(8, 8, 512) for part in parts], axis=1)
            pair = pair.reshape(8, 16, 512).astype(BF)
            for zb in range(8):
                cols[pl.ds((zb + 1) * 144 + (dy * 3 + dx) * 16, 16), :] = pair[zb]


def gather_terms(total, keep, gather):
    pieces = []
    total = total.reshape(8, 32, 432)
    for dz in range(3):
        kept = total[0] * keep[dz, 0:1, :]
        for zo in range(1, 8):
            kept = kept + total[zo] * keep[dz, zo : zo + 1, :]
        pieces.append(
            jnp.dot(kept, gather[...], preferred_element_type=F32, precision=lax.Precision.HIGHEST)
        )
    return pieces


def cascade(
    k_hbm, m_hbm, g_hbm, s_hbm, iy_hbm, fy_hbm, iz, fz, weight, w_in, bias, w_out, w_back, keep, gather,
    out_hbm, totals,
    kv, gv, mv, sens, iy, fy, stage, sk, sg, sf, rk, rg, rf,
    own_k, own_g, near_k, near_g, q_mid, q_send, q_near,
    cols, cols_g, hidden, slope, sum_in, sum_out, sum_b, first, second,
    load_sem, send_sem, recv_sem, store_sem,
):
    my_y, my_z = lax.axis_index("gy"), lax.axis_index("gz")
    me = my_y * 16 + my_z
    pos_x, pos_y, pos_z, pos_c = my_y % 4, my_y // 4 * 2 + my_z // 8, my_z // 2 % 4, my_z % 2
    left, right = (me + 127) % 128, (me + 1) % 128

    def pair(t):
        return (t // 16, t % 16)

    loads = [
        pltpu.make_async_copy(src, dst, load_sem.at[n])
        for n, (src, dst) in enumerate(
            [(k_hbm, kv), (g_hbm, gv), (iy_hbm, iy), (s_hbm, sens), (fy_hbm, fy), (m_hbm, mv)]
        )
    ]
    for load in loads:
        load.start()
    barrier = pltpu.get_barrier_semaphore()

    def greet(n):
        pl.semaphore_signal(barrier, inc=1, device_id=pair((me + n) % 128), device_id_type=MESH)

    def remote(src, dst, n, t):
        return pltpu.make_async_remote_copy(
            src_ref=src,
            dst_ref=dst,
            send_sem=send_sem.at[n],
            recv_sem=recv_sem.at[n],
            device_id=pair(t),
            device_id_type=MESH,
        )

    def target(i):
        n = i * 45 % 128
        x, y = (pos_x + n // 2 % 4) % 4, (pos_y + n // 8 % 4) % 4
        z, c = (pos_z + n // 32) % 4, (pos_c + n % 2) % 2
        return (y // 2 * 4 + x) * 16 + y % 2 * 8 + z * 2 + c

    def turn(source, index):
        depth, coil = index // 16, index % 16
        both = jnp.concatenate([source[0, coil, depth], source[1, coil, depth]], axis=0)
        stage[pl.ds(index, 128, stride=64), :] = both.astype(F32).T

    def block_of(t):
        return stage[pl.ds(pl.multiple_of(t * 64, 64), 64), :].astype(BF)

    loads[0].wait()
    turn(kv, 0)
    greet(64)

    def turn_k(index, carry):
        turn(kv, index)
        greet(index)
        greet(index + 64)
        return carry

    lax.fori_loop(1, 64, turn_k, 0)
    pl.semaphore_wait(barrier, 127)
    rk[me] = block_of(me)

    def send_k(i, carry):
        t = target(i)
        sk[t] = block_of(t)
        remote(sk.at[t], rk.at[me], 0, t).start()
        return carry

    lax.fori_loop(1, 128, send_k, 0)
    loads[1].wait()

    def turn_g(index, carry):
        turn(gv, index)
        return carry

    lax.fori_loop(0, 64, turn_g, 0, unroll=2)
    rg[me] = block_of(me)

    def send_g(i):
        t = target(i)
        remote(sg.at[t], rg.at[me], 1, t).start()

    def first_g(i, carry):
        t = target(i)
        sg[t] = block_of(t)
        send_g(i)
        return carry

    def keep_g(i, carry):
        t = target(i)
        sg[t] = block_of(t)
        return carry

    lax.fori_loop(1, BATCH_A, first_g, 0)
    lax.fori_loop(BATCH_A, 128, keep_g, 0, unroll=2)

    def wait_blocks(sent, got, n):
        every = pltpu.make_async_remote_copy(
            src_ref=sent.at[pl.ds(0, 127)],
            dst_ref=got.at[pl.ds(0, 127)],
            send_sem=send_sem.at[n],
            recv_sem=recv_sem.at[n],
            device_id=pair(right),
            device_id_type=MESH,
        )
        every.wait_send()
        every.wait_recv()

    def to_image(tiles, image):
        def rows(m, carry):
            lines = jnp.concatenate(
                [tiles[pl.ds(gy * 16 + m * 4, 4)].reshape(256, 128) for gy in range(8)], axis=1
            )
            done = jnp.dot(lines, iy[...], preferred_element_type=F32)
            for lt in range(8):
                span = pl.ds(pl.multiple_of(lt * 1024 + m * 256, 256), 256)
                stage[span, :] = done[:, lt * 128 : lt * 128 + 128]
            return carry

        lax.fori_loop(0, 4, rows, 0)

        def coil(c, carry):
            real, imag = carry
            lines = [stage[pl.ds(lt * 1024 + c, 64, stride=16), :].astype(BF) for lt in range(8)]
            lines = [jnp.concatenate(lines[4 * p : 4 * p + 4], axis=1) for p in range(2)]
            done = jnp.dot(iz[...], jnp.concatenate(lines, axis=0), preferred_element_type=F32)
            c_r, c_i = done[:64], done[64:]
            s_r, s_i = sens[0, 0, c].astype(F32), sens[1, 0, c].astype(F32)
            return real + (s_r * c_r + s_i * c_i), imag + (s_r * c_i - s_i * c_r)

        zero = jnp.zeros((64, 512), F32)
        real, imag = lax.fori_loop(0, 16, coil, (zero, zero))
        image[0] = real.astype(BF)
        image[1] = imag.astype(BF)

    def to_neighbours(up, down, near, n):
        copies = [remote(up, near.at[0], n, right), remote(down, near.at[1], n + 1, left)]
        for copy in copies:
            copy.start()
        return copies

    def beside(near, side, i):
        inside = me > 0 if side == 0 else me < 127
        return jnp.where(inside, near[side, i].astype(F32), 0.0)

    def three(own, near):
        return (
            lambda i: beside(near, 0, i),
            lambda i: own[i].astype(F32),
            lambda i: beside(near, 1, i),
        )

    loads[2].wait()
    loads[3].wait()
    wait_blocks(sk, rk, 0)
    to_image(rk, own_k)
    for copy in to_neighbours(own_k, own_k, near_k, 3):
        copy.wait()

    fill_columns(three(own_k, near_k), cols)
    hidden[pl.ds(0, 32), :] = jnp.zeros((32, 512), BF)
    hidden[pl.ds(65 * 32, 32), :] = jnp.zeros((32, 512), BF)

    def conv_in_block(zb, carry):
        for i in range(5):
            send_g(BATCH_A + zb * 5 + i)
        window = cols[pl.ds(pl.multiple_of(zb * 144, 16), 432), :]
        pre = jnp.dot(w_in[...], window, preferred_element_type=F32) + bias[...]
        sig = jax.nn.sigmoid(pre)
        hidden[pl.ds(pl.multiple_of(zb * 256 + 32, 32), 256), :] = (pre * sig).astype(BF)
        slope[pl.ds(pl.multiple_of(zb * 256, 256), 256), :] = sig * (1.0 + pre * (1.0 - sig))
        return carry

    lax.fori_loop(0, 8, conv_in_block, 0)

    def conv_out_block(zb, carry):
        window = hidden[pl.ds(pl.multiple_of(zb * 256, 256), 320), :]
        terms = jnp.dot(w_out[...], window, preferred_element_type=F32).reshape(18, 8, 512)
        rows = pl.ds(pl.multiple_of(zb * 8, 8), 8)
        for dx in range(3):
            for o in range(2):
                base = (dx * 2 + o) * 3
                total = shifted(terms[base], 0) + terms[base + 1] + shifted(terms[base + 2], 2)
                q_mid[dx, o, rows, :] = total
        return carry

    lax.fori_loop(0, 8, conv_out_block, 0)
    q_send[0] = q_mid[0].astype(BF)
    q_send[1] = q_mid[2].astype(BF)
    for copy in to_neighbours(q_send.at[0], q_send.at[1], q_near, 5):
        copy.wait()

    r_r, r_i = [
        (beside(q_near, 0, o) + q_mid[1, o] + beside(q_near, 1, o)).astype(BF).astype(F32)
        for o in range(2)
    ]

    def spread(c, carry):
        for i in range(3):
            send_g(BATCH_A + 40 + c * 3 + i)
        s_r, s_i = sens[0, 0, c].astype(F32), sens[1, 0, c].astype(F32)
        lines = jnp.concatenate([s_r * r_r - s_i * r_i, s_r * r_i + s_i * r_r], axis=0).astype(BF)
        done = jnp.dot(fz[...], lines, preferred_element_type=F32)
        for lt in range(8):
            p, lane = lt // 4, lt % 4 * 128
            stage[pl.ds(lt * 1024 + c, 64, stride=16), :] = done[p * 64 : p * 64 + 64, lane : lane + 128]
        return carry

    lax.fori_loop(0, 16, spread, 0)
    loads[4].wait()

    def send_f(step, carry):
        m = (step + my_z // 4) % 4
        lines = [stage[pl.ds(pl.multiple_of(lt * 1024 + m * 256, 256), 256), :] for lt in range(8)]
        lines = jnp.concatenate([part.astype(BF) for part in lines], axis=1)
        done = jnp.dot(lines, fy[...], preferred_element_type=F32).astype(BF)
        for gy in range(8):
            sf[pl.ds(gy * 16 + m * 4, 4)] = done[:, gy * 128 : gy * 128 + 128].reshape(4, 64, 128)

        def start(j, inner):
            t = (my_y + j % 8) % 8 * 16 + m * 4 + (my_z + j // 8) % 4

            @pl.when(t != me)
            def _():
                remote(sf.at[t], rf.at[me], 2, t).start()

            return inner

        lax.fori_loop(0, 32, start, 0)
        return carry

    lax.fori_loop(0, 4, send_f, 0)
    rf[me] = sf[me]

    wait_blocks(sg, rg, 1)
    to_image(rg, own_g)
    for copy in to_neighbours(own_g, own_g, near_g, 7):
        copy.wait()
    fill_columns(three(own_g, near_g), cols_g)
    sum_in[...] = jnp.zeros_like(sum_in)
    sum_out[...] = jnp.zeros_like(sum_out)
    sum_b[...] = jnp.zeros_like(sum_b)
    nt = (((1,), (1,)), ((), ()))

    def back_block(zb, carry):
        span = pl.ds(pl.multiple_of(zb * 144, 16), 432)
        window_g = cols_g[span, :]
        back = jnp.dot(w_back[...], window_g, preferred_element_type=F32)
        back = (back * slope[pl.ds(pl.multiple_of(zb * 256, 256), 256), :]).astype(BF)
        sum_in[...] += lax.dot_general(back, cols[span, :], nt, preferred_element_type=F32)
        held = hidden[pl.ds(pl.multiple_of(zb * 256 + 32, 32), 256), :]
        sum_out[...] += lax.dot_general(held, window_g, nt, preferred_element_type=F32)
        wide = back.astype(F32)
        sum_b[...] += wide[:, :128] + wide[:, 128:256] + wide[:, 256:384] + wide[:, 384:]
        return carry

    lax.fori_loop(0, 8, back_block, 0)
    bias_sum = jnp.sum(sum_b[...].reshape(8, 32, 128), axis=0)
    bias_sum = jnp.sum(bias_sum, axis=1, keepdims=True)
    pieces = gather_terms(sum_in[...], keep, gather) + gather_terms(sum_out[...], keep, gather)
    pieces.append(jnp.broadcast_to(bias_sum, (32, 20)))

    def share(buffer, mine, count, n, device):
        def start(step, carry):
            remote(buffer.at[mine], buffer.at[mine], n, device((mine + step) % count)).start()
            return carry

        lax.fori_loop(1, count, start, 0)

    def collect(buffer, count, n):
        every = pltpu.make_async_remote_copy(
            src_ref=buffer.at[pl.ds(0, count - 1)],
            dst_ref=buffer.at[pl.ds(0, count - 1)],
            send_sem=send_sem.at[n],
            recv_sem=recv_sem.at[n],
            device_id=pair(right),
            device_id_type=MESH,
        )
        every.wait_send()
        every.wait_recv()
        total = buffer[0]
        for index in range(1, count):
            total = total + buffer[index]
        return total

    first[my_z] = jnp.concatenate(pieces, axis=1)
    share(first, my_z, 16, 9, lambda to: my_y * 16 + to)

    loads[5].wait()
    wait_blocks(sf, rf, 2)

    def widen(x, carry):
        stage[pl.ds(pl.multiple_of(x * 64, 64), 64), :] = rf[x].astype(F32)
        return carry

    lax.fori_loop(0, 128, widen, 0, unroll=4)
    second[my_y] = collect(first, 16, 9)
    share(second, my_y, 8, 10, lambda to: to * 16 + my_z)

    def finish(index, carry):
        depth, coil = index // 16, index % 16
        both = stage[pl.ds(index, 128, stride=64), :].T
        part_of = weight[depth]
        for part in range(2):
            current = kv[part, coil, depth].astype(F32)
            other = mv[part, coil, depth].astype(F32)
            refine = both[part * 64 : part * 64 + 64]
            kv[part, coil, depth] = (current - part_of * (current - other) + refine).astype(BF)
        return carry

    stores = []
    for depth in range(4):
        lax.fori_loop(depth * 16, depth * 16 + 16, finish, 0, unroll=2)
        stores.append(
            pltpu.make_async_copy(kv.at[:, :, depth], out_hbm.at[:, :, depth], store_sem.at[depth])
        )
        stores[-1].start()
    totals[...] = collect(second, 8, 10)
    for store in stores:
        store.wait()


def run_cascade(*operands):
    blocks = pltpu.VMEM((128, 64, 128), BF)
    tile = pltpu.VMEM((2, 16, 4, 64, 128), BF)
    image = pltpu.VMEM((2, 64, 512), BF)
    near = pltpu.VMEM((2, 2, 64, 512), BF)
    table = pltpu.VMEM((1024, 1024), BF)
    hbm = pl.BlockSpec(memory_space=pl.ANY)
    return pl.pallas_call(
        cascade,
        out_shape=(
            jax.ShapeDtypeStruct((2, 16, 4, 64, 128), BF),
            jax.ShapeDtypeStruct((32, 128), F32),
        ),
        in_specs=[hbm] * 6 + [VM] * 9,
        out_specs=(hbm, VM),
        scratch_shapes=[
            tile, tile, tile,
            pltpu.VMEM((2, 1, 16, 64, 512), BF),
            table, table,
            pltpu.VMEM((8192, 128), F32),
            blocks, blocks, blocks, blocks, blocks, blocks,
            image, image, near, near,
            pltpu.VMEM((3, 2, 64, 512), F32),
            near, near,
            pltpu.VMEM((1440, 512), BF),
            pltpu.VMEM((1440, 512), BF),
            pltpu.VMEM((66 * 32, 512), BF),
            pltpu.VMEM((2048, 512), F32),
            pltpu.VMEM((256, 432), F32),
            pltpu.VMEM((256, 432), F32),
            pltpu.VMEM((256, 128), F32),
            pltpu.VMEM((16, 32, 128), F32),
            pltpu.VMEM((8, 32, 128), F32),
            pltpu.SemaphoreType.DMA((6,)),
            pltpu.SemaphoreType.DMA((11,)),
            pltpu.SemaphoreType.DMA((11,)),
            pltpu.SemaphoreType.DMA((4,)),
        ],
        compiler_params=pltpu.CompilerParams(
            collective_id=0, has_side_effects=True, vmem_limit_bytes=VMEM_LIMIT
        ),
        name="cascade",
    )(*operands)


def on_device(
    kspace, measured, sample_mask, step_size, coil_field, conv_in, bias_in, conv_out, cotangent
):
    count_y, count_z = lax.axis_size("gy"), lax.axis_size("gz")
    row_tile, x_cells, depth_tile = kspace.shape[3], kspace.shape[4], kspace.shape[2]
    inverse_y = jnp.asarray(inverse_y_table(count_y, row_tile))
    forward_y = jnp.asarray(forward_y_table(count_y, row_tile))
    inverse_z = jnp.asarray(z_table(count_z * depth_tile, True))
    forward_z = jnp.asarray(z_table(count_z * depth_tile, False))
    spread = jnp.asarray(band_spread())
    keep = jnp.asarray(band_keep())
    gather = jnp.asarray(band_gather())
    spread_out = jnp.asarray(out_spread())

    flat_in = conv_in.transpose(0, 2, 3, 4, 1).reshape(32, 54)
    w_in = jnp.einsum("ok,zkc->zoc", flat_in, spread).reshape(256, 432)
    flat_back = conv_out[:, :, ::-1, ::-1, ::-1].transpose(1, 2, 3, 4, 0).reshape(32, 54)
    w_back = jnp.einsum("ok,zkc->zoc", flat_back, spread).reshape(256, 432)
    flat_out = conv_out.transpose(1, 2, 4, 0, 3).reshape(32, 54)
    w_out = jnp.einsum("ik,qkr->rqi", flat_out, spread_out).reshape(144, 320)
    bias = jnp.tile(bias_in, 8)[:, None]
    weight = jnp.broadcast_to(
        (step_size[0] * sample_mask.astype(F32))[:, :, None], (depth_tile, row_tile, x_cells)
    )

    kspace_next, totals = run_cascade(
        kspace, measured, cotangent, coil_field, inverse_y, forward_y, inverse_z, forward_z,
        weight, w_in, bias, w_out, w_back, keep, gather,
    )

    norm = 1.0 / math.sqrt(x_cells * row_tile * count_y * depth_tile * count_z)
    totals = totals * norm
    grad_in = totals[:, :54].reshape(32, 3, 3, 3, 2).transpose(0, 4, 1, 2, 3)
    grad_out = totals[:, 54:108].reshape(32, 3, 3, 3, 2).transpose(4, 0, 1, 2, 3)
    grad_out = grad_out[:, :, ::-1, ::-1, ::-1]
    return kspace_next, grad_in, totals[:, 108], grad_out


def solution(mesh):
    tile = P(None, None, "gz", "gy", None)
    in_specs = (
        tile,
        tile,
        P("gz", "gy"),
        P(),
        P(None, AXES, None, None, None),
        P(),
        P(),
        P(),
        tile,
    )
    out_specs = (tile, P(), P(), P())
    return jax.shard_map(
        on_device, mesh=mesh, in_specs=in_specs, out_specs=out_specs, check_vma=False
    )
```

```python
import functools
import math

import jax
import jax.numpy as jnp
import numpy as np
from jax import lax
from jax.experimental import pallas as pl
from jax.experimental.pallas import tpu as pltpu
from jax.sharding import PartitionSpec as P

MESH = pl.DeviceIdType.MESH
AXES = ("gy", "gz")
BF = jnp.bfloat16
F32 = jnp.float32
VMEM_LIMIT = 56 * 2**20
VM = pl.BlockSpec(memory_space=pltpu.VMEM)


def trig(length):
    index = np.arange(length, dtype=np.int64)
    angle = (index[:, None] * index[None, :] % length).astype(np.float64) * (2.0 * math.pi / length)
    factor = 1.0 / math.sqrt(length)
    return np.cos(angle) * factor, np.sin(angle) * factor


def as_bf16(array):
    return np.asarray(array, dtype=np.float32).astype(jnp.bfloat16)


def inverse_y_table(gy, rows):
    length = gy * rows
    cos, sin = trig(length)
    cos, sin = cos.reshape(gy, rows, length), sin.reshape(gy, rows, length)
    table = np.stack([np.stack([cos, sin], 2), np.stack([-sin, cos], 2)], 1)
    return as_bf16(table.reshape(2 * length, 2 * length))


def forward_y_table(gy, rows):
    length = gy * rows
    cos, sin = trig(length)
    cos, sin = cos.reshape(length, gy, rows), sin.reshape(length, gy, rows)
    table = np.stack([np.stack([cos, -sin], 2), np.stack([sin, cos], 2)], 0)
    return as_bf16(table.reshape(2 * length, 2 * length))


def z_table(length, inverse):
    cos, sin = trig(length)
    if inverse:
        table = np.block([[cos, -sin], [sin, cos]])
    else:
        table = np.block([[cos, sin], [-sin, cos]])
    return as_bf16(table)


def band_masks():
    zo, dz, j, zi = np.ogrid[0:8, 0:3, 0:3, 0:8]
    return (8 * (j - 1) + zi == zo + dz - 1).astype(np.float32)


def band_spread():
    hit = band_masks()
    eye = np.eye(18, dtype=np.float32)
    spread = np.einsum("odjz,kl->odkjlz", hit, eye)
    return as_bf16(spread.reshape(8, 54, 432))


def band_keep():
    hit = band_masks()
    keep = np.broadcast_to(hit.transpose(1, 0, 2, 3)[:, :, :, None, :], (3, 8, 3, 18, 8))
    return np.ascontiguousarray(keep.reshape(3, 8, 432)).astype(np.float32)


def band_spread_flipped():
    spread = band_spread().reshape(8, 3, 3, 3, 2, 432)
    return np.ascontiguousarray(spread[:, ::-1, ::-1, ::-1].reshape(8, 54, 432))


def band_gather():
    eye = np.eye(18, dtype=np.float32)
    both = np.stack([eye, eye.reshape(18, 3, 3, 2)[:, ::-1, ::-1].reshape(18, 18)])
    both = np.broadcast_to(both[:, None, :, None, :], (2, 3, 18, 8, 18))
    return np.ascontiguousarray(both.reshape(2, 432, 18))


def out_spread():
    q, dz, zo = np.ogrid[0:10, 0:3, 0:8]
    hit = (q == zo + dz).astype(np.float32)
    three, two = np.eye(3, dtype=np.float32), np.eye(2, dtype=np.float32)
    spread = np.einsum("qdz,yY,xX,oO->qdyxoXOYz", hit, three, three, two)
    return as_bf16(spread.reshape(10, 54, 144))


BATCH = 64


def shifted(value, dy):
    if dy == 1:
        return value
    lane = lax.broadcasted_iota(jnp.int32, value.shape, value.ndim - 1)
    if dy == 0:
        return jnp.where(lane == 0, 0.0, pltpu.roll(value, 1, value.ndim - 1))
    return jnp.where(lane == 511, 0.0, pltpu.roll(value, 511, value.ndim - 1))


def fill_columns(images, cols):
    cols[pl.ds(0, 144), :] = jnp.zeros((144, 512), BF)
    cols[pl.ds(1296, 144), :] = jnp.zeros((144, 512), BF)
    for dx, image in enumerate(images):
        parts = [image(i) for i in range(2)]
        for dy in range(3):
            pair = jnp.stack([shifted(part, dy).reshape(8, 8, 512) for part in parts], axis=1)
            pair = pair.reshape(8, 16, 512).astype(BF)
            for zb in range(8):
                cols[pl.ds((zb + 1) * 144 + (dy * 3 + dx) * 16, 16), :] = pair[zb]


def gather_terms(total, keep, gather, order):
    pieces = []
    total = total.reshape(8, 32, 432)
    for dz in order:
        kept = total[0] * keep[dz, 0:1, :]
        for zo in range(1, 8):
            kept = kept + total[zo] * keep[dz, zo : zo + 1, :]
        pieces.append(
            jnp.dot(kept, gather, preferred_element_type=F32, precision=lax.Precision.HIGHEST)
        )
    return pieces


def cascade(
    norm,
    k_hbm, m_hbm, g_hbm, s_hbm, iy_hbm, fy_hbm, spread_in_hbm, spread_back_hbm, spread_out_hbm,
    iz, fz, mask, step, flat_in, bias, flat_out, keep, gather,
    out_hbm, grad_in, grad_bias, grad_out,
    kv, gv, mv, sens, iy, fy, stage, sk, sg, sf, rk, rg, rf,
    own_k, own_g, near_k, near_g, q_mid, q_send, q_near,
    cols, cols_g, hidden, slope, sum_in, sum_out, sum_b, first, second,
    weight, bias_cols, w_in, w_back, w_out, spread_in, spread_back, spread_out,
    load_sem, send_sem, recv_sem, store_sem,
):
    my_y, my_z = lax.axis_index("gy"), lax.axis_index("gz")
    me = my_y * 16 + my_z
    pos_x, pos_y, pos_z, pos_c = my_y % 4, my_y // 4 * 2 + my_z // 8, my_z // 2 % 4, my_z % 2
    left, right = (me + 127) % 128, (me + 1) % 128

    def pair(t):
        return (lax.div(t, 16), lax.rem(t, 16))

    loads = [
        pltpu.make_async_copy(src, dst, load_sem.at[n])
        for n, (src, dst) in enumerate(
            [(k_hbm, kv), (g_hbm, gv), (iy_hbm, iy), (s_hbm, sens), (fy_hbm, fy), (m_hbm, mv),
             (spread_in_hbm, spread_in), (spread_back_hbm, spread_back), (spread_out_hbm, spread_out)]
        )
    ]
    for load in loads:
        load.start()
    barrier = pltpu.get_barrier_semaphore()

    def greet(n, carry):
        pl.semaphore_signal(barrier, inc=1, device_id=pair(lax.rem(me + n, 128)), device_id_type=MESH)
        return carry

    lax.fori_loop(1, 128, greet, 0)

    def remote(src, dst, n, t):
        return pltpu.make_async_remote_copy(
            src_ref=src,
            dst_ref=dst,
            send_sem=send_sem.at[n],
            recv_sem=recv_sem.at[n],
            device_id=pair(t),
            device_id_type=MESH,
        )

    def target(i):
        n = lax.rem(i * 45, 128)
        x = lax.rem(pos_x + lax.rem(lax.div(n, 2), 4), 4)
        y = lax.rem(pos_y + lax.rem(lax.div(n, 8), 4), 4)
        z = lax.rem(pos_z + lax.div(n, 32), 4)
        c = lax.rem(pos_c + lax.rem(n, 2), 2)
        return (lax.div(y, 2) * 4 + x) * 16 + lax.rem(y, 2) * 8 + z * 2 + c

    def turn(source, index):
        depth, coil = index // 16, index % 16
        both = jnp.concatenate([source[0, coil, depth], source[1, coil, depth]], axis=0)
        stage[pl.ds(index, 128, stride=64), :] = both.T.astype(F32)

    def block_of(t):
        return stage[pl.ds(pl.multiple_of(t * 64, 64), 64), :].astype(BF)

    def turn_k(index, carry):
        turn(kv, index)
        return carry

    def send_k(i, carry):
        t = target(i)
        sk[t] = block_of(t)
        remote(sk.at[t], rk.at[me], 0, t).start()
        return carry

    loads[0].wait()
    lax.fori_loop(0, 64, turn_k, 0, unroll=2)
    pl.semaphore_wait(barrier, 127)
    rk[me] = block_of(me)
    lax.fori_loop(1, 128, send_k, 0)

    def turn_g(index, carry):
        turn(gv, index)
        return carry

    def first_g(i, carry):
        t = target(i)
        sg[t] = block_of(t)
        remote(sg.at[t], rg.at[me], 1, t).start()
        return carry

    def keep_g(i, carry):
        t = target(i)
        sg[t] = block_of(t)
        return carry

    def later_g(i, carry):
        t = target(i)
        remote(sg.at[t], rg.at[me], 1, t).start()
        return carry

    loads[1].wait()
    lax.fori_loop(0, 64, turn_g, 0, unroll=2)
    rg[me] = block_of(me)
    lax.fori_loop(1, BATCH, first_g, 0)
    lax.fori_loop(BATCH, 128, keep_g, 0, unroll=2)

    for n in (6, 7, 8):
        loads[n].wait()
    contract = (((0,), (0,)), ((), ()))
    for zo in range(8):
        rows = pl.ds(zo * 32, 32)
        band = lax.dot_general(flat_in[...], spread_in[zo], contract, preferred_element_type=F32)
        w_in[rows, :] = band.astype(BF)
        band = lax.dot_general(flat_out[...], spread_back[zo], contract, preferred_element_type=F32)
        w_back[rows, :] = band.astype(BF)
    bands = [
        lax.dot_general(spread_out[q], flat_out[...], contract, preferred_element_type=F32)
        for q in range(10)
    ]
    w_out[...] = jnp.concatenate(bands, axis=1).astype(BF)

    def upright(row):
        return jnp.broadcast_to(row, (128, 128)).T

    bias_rows = upright(jnp.concatenate([bias[...]] * 4, axis=1))[:32]
    for zo in range(8):
        bias_cols[pl.ds(zo * 32, 32), :] = bias_rows
    for depth in range(4):
        row = mask[pl.ds(depth, 1), :].astype(F32) * step[...]
        weight[depth] = upright(jnp.concatenate([row, row], axis=1))[:64]

    def wait_blocks(sent, got, n):
        every = pltpu.make_async_remote_copy(
            src_ref=sent.at[pl.ds(0, 127)],
            dst_ref=got.at[pl.ds(0, 127)],
            send_sem=send_sem.at[n],
            recv_sem=recv_sem.at[n],
            device_id=pair(right),
            device_id_type=MESH,
        )
        every.wait_send()
        every.wait_recv()

    def to_image(tiles, image):
        def rows(m, carry):
            lines = jnp.concatenate(
                [tiles[pl.ds(gy * 16 + m * 4, 4)].reshape(256, 128) for gy in range(8)], axis=1
            )
            done = jnp.dot(lines, iy[...], preferred_element_type=F32)
            for lt in range(8):
                span = pl.ds(pl.multiple_of(lt * 1024 + m * 256, 256), 256)
                stage[span, :] = done[:, lt * 128 : lt * 128 + 128]
            return carry

        lax.fori_loop(0, 4, rows, 0)

        for chunk in range(4):
            lane = pl.ds(chunk * 128, 128)

            def coils(step_c, carry):
                real, imag = carry
                lines = []
                for c in (2 * step_c, 2 * step_c + 1):
                    halves = [
                        stage[pl.ds((p * 4 + chunk) * 1024 + c, 64, stride=16), :] for p in range(2)
                    ]
                    lines.append(jnp.concatenate(halves, axis=0).astype(BF))
                done = jnp.dot(
                    iz[...], jnp.concatenate(lines, axis=1), preferred_element_type=F32
                )
                for k in range(2):
                    c = 2 * step_c + k
                    c_r, c_i = done[:64, k * 128 : k * 128 + 128], done[64:, k * 128 : k * 128 + 128]
                    s_r, s_i = sens[0, 0, c, :, lane].astype(F32), sens[1, 0, c, :, lane].astype(F32)
                    real = real + (s_r * c_r + s_i * c_i)
                    imag = imag + (s_r * c_i - s_i * c_r)
                return real, imag

            zero = jnp.zeros((64, 128), F32)
            real, imag = lax.fori_loop(0, 8, coils, (zero, zero), unroll=2)
            image[0, :, lane] = real.astype(BF)
            image[1, :, lane] = imag.astype(BF)

    def to_neighbours(up, down, near, n):
        copies = [remote(up, near.at[0], n, right), remote(down, near.at[1], n + 1, left)]
        for copy in copies:
            copy.start()
        return copies

    def beside(near, side, i):
        inside = me > 0 if side == 0 else me < 127
        return jnp.where(inside, near[side, i].astype(F32), 0.0)

    def three(own, near):
        return (
            lambda i: beside(near, 0, i),
            lambda i: own[i].astype(F32),
            lambda i: beside(near, 1, i),
        )

    loads[2].wait()
    loads[3].wait()
    wait_blocks(sk, rk, 0)
    to_image(rk, own_k)
    copies = to_neighbours(own_k, own_k, near_k, 3)
    lax.fori_loop(BATCH, 128, later_g, 0)
    for copy in copies:
        copy.wait()

    fill_columns(three(own_k, near_k), cols)
    hidden[pl.ds(0, 32), :] = jnp.zeros((32, 512), BF)
    hidden[pl.ds(65 * 32, 32), :] = jnp.zeros((32, 512), BF)

    def conv_in_block(zb, carry):
        window = cols[pl.ds(pl.multiple_of(zb * 144, 16), 432), :]
        pre = jnp.dot(w_in[...], window, preferred_element_type=F32)
        pre = pre + jnp.concatenate([bias_cols[...]] * 4, axis=1)
        sig = jax.nn.sigmoid(pre)
        hidden[pl.ds(pl.multiple_of(zb * 256 + 32, 32), 256), :] = (pre * sig).astype(BF)
        slope[pl.ds(pl.multiple_of(zb * 256, 256), 256), :] = sig * (1.0 + pre * (1.0 - sig))
        return carry

    lax.fori_loop(0, 8, conv_in_block, 0)

    def conv_out_block(zb, carry):
        window = hidden[pl.ds(pl.multiple_of(zb * 256, 256), 320), :]
        terms = jnp.dot(w_out[...], window, preferred_element_type=F32).reshape(18, 8, 512)
        rows = pl.ds(pl.multiple_of(zb * 8, 8), 8)
        for dx in range(3):
            for o in range(2):
                base = (dx * 2 + o) * 3
                total = shifted(terms[base], 0) + terms[base + 1] + shifted(terms[base + 2], 2)
                q_mid[dx, o, rows, :] = total
        return carry

    lax.fori_loop(0, 8, conv_out_block, 0)
    q_send[0] = q_mid[0].astype(BF)
    q_send[1] = q_mid[2].astype(BF)
    q_copies = to_neighbours(q_send.at[0], q_send.at[1], q_near, 5)

    wait_blocks(sg, rg, 1)
    to_image(rg, own_g)
    g_copies = to_neighbours(own_g, own_g, near_g, 7)
    for copy in q_copies:
        copy.wait()

    for o in range(2):
        total = beside(q_near, 0, o) + q_mid[1, o] + beside(q_near, 1, o)
        q_mid[0, o] = total.astype(BF).astype(F32)
    for chunk in range(4):
        lane = pl.ds(chunk * 128, 128)
        r_r, r_i = q_mid[0, 0, :, lane], q_mid[0, 1, :, lane]

        def spread(step_c, carry):
            lines = []
            for c in (2 * step_c, 2 * step_c + 1):
                s_r, s_i = sens[0, 0, c, :, lane].astype(F32), sens[1, 0, c, :, lane].astype(F32)
                both = [s_r * r_r - s_i * r_i, s_r * r_i + s_i * r_r]
                lines.append(jnp.concatenate(both, axis=0).astype(BF))
            done = jnp.dot(fz[...], jnp.concatenate(lines, axis=1), preferred_element_type=F32)
            for k in range(2):
                for p in range(2):
                    rows = pl.ds((p * 4 + chunk) * 1024 + 2 * step_c + k, 64, stride=16)
                    stage[rows, :] = done[p * 64 : p * 64 + 64, k * 128 : k * 128 + 128]
            return carry

        lax.fori_loop(0, 8, spread, 0, unroll=2)
    loads[4].wait()

    def send_f(step, carry):
        m = (step + my_z // 4) % 4
        lines = [stage[pl.ds(pl.multiple_of(lt * 1024 + m * 256, 256), 256), :] for lt in range(8)]
        lines = jnp.concatenate([part.astype(BF) for part in lines], axis=1)
        done = jnp.dot(lines, fy[...], preferred_element_type=F32).astype(BF)
        for gy in range(8):
            sf[pl.ds(gy * 16 + m * 4, 4)] = done[:, gy * 128 : gy * 128 + 128].reshape(4, 64, 128)

        def start(j, inner):
            t = (my_y + j % 8) % 8 * 16 + m * 4 + (my_z + j // 8) % 4

            @pl.when(t != me)
            def _():
                remote(sf.at[t], rf.at[me], 2, t).start()

            return inner

        lax.fori_loop(0, 32, start, 0)
        return carry

    lax.fori_loop(0, 4, send_f, 0)
    rf[me] = sf[me]

    for copy in g_copies:
        copy.wait()
    fill_columns(three(own_g, near_g), cols_g)
    sum_in[...] = jnp.zeros_like(sum_in)
    sum_out[...] = jnp.zeros_like(sum_out)
    sum_b[...] = jnp.zeros_like(sum_b)
    nt = (((1,), (1,)), ((), ()))

    def back_block(zb, carry):
        span = pl.ds(pl.multiple_of(zb * 144, 16), 432)
        window_g = cols_g[span, :]
        back = jnp.dot(w_back[...], window_g, preferred_element_type=F32)
        back = (back * slope[pl.ds(pl.multiple_of(zb * 256, 256), 256), :]).astype(BF)
        sum_in[...] += lax.dot_general(back, cols[span, :], nt, preferred_element_type=F32)
        held = hidden[pl.ds(pl.multiple_of(zb * 256 + 32, 32), 256), :]
        sum_out[...] += lax.dot_general(held, window_g, nt, preferred_element_type=F32)
        wide = back.astype(F32)
        sum_b[...] += wide[:, :128] + wide[:, 128:256] + wide[:, 256:384] + wide[:, 384:]
        return carry

    lax.fori_loop(0, 8, back_block, 0)
    bias_sum = jnp.sum(sum_b[...].reshape(8, 32, 128), axis=0)
    bias_sum = jnp.sum(bias_sum, axis=1, keepdims=True)
    pieces = gather_terms(sum_in[...], keep, gather[0], (0, 1, 2))
    pieces += gather_terms(sum_out[...], keep, gather[1], (2, 1, 0))
    pieces.append(jnp.broadcast_to(bias_sum, (32, 20)))

    def share(buffer, mine, count, n, device):
        def start(step, carry):
            remote(buffer.at[mine], buffer.at[mine], n, device((mine + step) % count)).start()
            return carry

        lax.fori_loop(1, count, start, 0)

    def collect(buffer, count, n):
        every = pltpu.make_async_remote_copy(
            src_ref=buffer.at[pl.ds(0, count - 1)],
            dst_ref=buffer.at[pl.ds(0, count - 1)],
            send_sem=send_sem.at[n],
            recv_sem=recv_sem.at[n],
            device_id=pair(right),
            device_id_type=MESH,
        )
        every.wait_send()
        every.wait_recv()
        total = buffer[0]
        for index in range(1, count):
            total = total + buffer[index]
        return total

    first[my_z] = jnp.concatenate(pieces, axis=1)
    share(first, my_z, 16, 9, lambda to: my_y * 16 + to)

    loads[5].wait()
    wait_blocks(sf, rf, 2)

    def widen(x, carry):
        stage[pl.ds(pl.multiple_of(x * 64, 64), 64), :] = rf[x].astype(F32)
        return carry

    lax.fori_loop(0, 128, widen, 0, unroll=4)
    second[my_y] = collect(first, 16, 9)
    share(second, my_y, 8, 10, lambda to: to * 16 + my_z)

    def finish(index, carry):
        depth, coil = index // 16, index % 16
        both = stage[pl.ds(index, 128, stride=64), :].astype(BF).T.astype(F32)
        part_of = weight[depth]
        for part in range(2):
            current = kv[part, coil, depth].astype(F32)
            other = mv[part, coil, depth].astype(F32)
            refine = both[part * 64 : part * 64 + 64]
            kv[part, coil, depth] = (current - part_of * (current - other) + refine).astype(BF)
        return carry

    stores = []
    for depth in range(4):
        lax.fori_loop(depth * 16, depth * 16 + 16, finish, 0, unroll=2)
        stores.append(
            pltpu.make_async_copy(kv.at[:, :, depth], out_hbm.at[:, :, depth], store_sem.at[depth])
        )
        stores[-1].start()
    total = jnp.concatenate([collect(second, 8, 10) * norm] * 4, axis=0).T[:, :32]
    grad_in[...] = total[:54]
    grad_out[...] = total[54:108]
    grad_bias[...] = total[108:109]
    for store in stores:
        store.wait()


def run_cascade(norm, *operands):
    blocks = pltpu.VMEM((128, 64, 128), BF)
    tile = pltpu.VMEM((2, 16, 4, 64, 128), BF)
    image = pltpu.VMEM((2, 64, 512), BF)
    near = pltpu.VMEM((2, 2, 64, 512), BF)
    table = pltpu.VMEM((1024, 1024), BF)
    hbm = pl.BlockSpec(memory_space=pl.ANY)
    return pl.pallas_call(
        functools.partial(cascade, norm),
        out_shape=(
            jax.ShapeDtypeStruct((2, 16, 4, 64, 128), BF),
            jax.ShapeDtypeStruct((54, 32), F32),
            jax.ShapeDtypeStruct((1, 32), F32),
            jax.ShapeDtypeStruct((54, 32), F32),
        ),
        in_specs=[hbm] * 9 + [VM] * 9,
        out_specs=(hbm, VM, VM, VM),
        scratch_shapes=[
            tile, tile, tile,
            pltpu.VMEM((2, 1, 16, 64, 512), BF),
            table, table,
            pltpu.VMEM((8192, 128), F32),
            blocks, blocks, blocks, blocks, blocks, blocks,
            image, image, near, near,
            pltpu.VMEM((3, 2, 64, 512), F32),
            near, near,
            pltpu.VMEM((1440, 512), BF),
            pltpu.VMEM((1440, 512), BF),
            pltpu.VMEM((66 * 32, 512), BF),
            pltpu.VMEM((2048, 512), F32),
            pltpu.VMEM((256, 432), F32),
            pltpu.VMEM((256, 432), F32),
            pltpu.VMEM((256, 128), F32),
            pltpu.VMEM((16, 32, 128), F32),
            pltpu.VMEM((8, 32, 128), F32),
            pltpu.VMEM((4, 64, 128), F32),
            pltpu.VMEM((256, 128), F32),
            pltpu.VMEM((256, 432), BF),
            pltpu.VMEM((256, 432), BF),
            pltpu.VMEM((144, 320), BF),
            pltpu.VMEM((8, 54, 432), BF),
            pltpu.VMEM((8, 54, 432), BF),
            pltpu.VMEM((10, 54, 144), BF),
            pltpu.SemaphoreType.DMA((9,)),
            pltpu.SemaphoreType.DMA((11,)),
            pltpu.SemaphoreType.DMA((11,)),
            pltpu.SemaphoreType.DMA((4,)),
        ],
        compiler_params=pltpu.CompilerParams(
            collective_id=0, has_side_effects=True, vmem_limit_bytes=VMEM_LIMIT
        ),
        name="cascade",
    )(*operands)


def on_device(
    kspace, measured, sample_mask, step_size, coil_field, conv_in, bias_in, conv_out, cotangent
):
    count_y, count_z = lax.axis_size("gy"), lax.axis_size("gz")
    row_tile, x_cells, depth_tile = kspace.shape[3], kspace.shape[4], kspace.shape[2]
    inverse_y = jnp.asarray(inverse_y_table(count_y, row_tile))
    forward_y = jnp.asarray(forward_y_table(count_y, row_tile))
    inverse_z = jnp.asarray(z_table(count_z * depth_tile, True))
    forward_z = jnp.asarray(z_table(count_z * depth_tile, False))
    norm = 1.0 / math.sqrt(x_cells * row_tile * count_y * depth_tile * count_z)
    kspace_next, grad_in, grad_bias, grad_out = run_cascade(
        norm, kspace, measured, cotangent, coil_field, inverse_y, forward_y,
        jnp.asarray(band_spread()), jnp.asarray(band_spread_flipped()), jnp.asarray(out_spread()),
        inverse_z, forward_z, sample_mask, step_size.reshape(1, 1),
        conv_in.transpose(2, 3, 4, 1, 0).reshape(54, 32), bias_in.reshape(1, 32),
        conv_out.transpose(2, 3, 4, 0, 1).reshape(54, 32),
        jnp.asarray(band_keep()), jnp.asarray(band_gather()),
    )
    grad_in = grad_in.reshape(3, 3, 3, 2, 32).transpose(4, 3, 0, 1, 2)
    grad_out = grad_out.reshape(3, 3, 3, 2, 32).transpose(3, 4, 0, 1, 2)
    return kspace_next, grad_in, grad_bias.reshape(32), grad_out


def solution(mesh):
    tile = P(None, None, "gz", "gy", None)
    in_specs = (
        tile,
        tile,
        P("gz", "gy"),
        P(),
        P(None, AXES, None, None, None),
        P(),
        P(),
        P(),
        tile,
    )
    out_specs = (tile, P(), P(), P())
    return jax.shard_map(
        on_device, mesh=mesh, in_specs=in_specs, out_specs=out_specs, check_vma=False
    )
```

```python
import functools
import math

import jax
import jax.numpy as jnp
import numpy as np
from jax import lax
from jax.experimental import pallas as pl
from jax.experimental.pallas import tpu as pltpu
from jax.sharding import PartitionSpec as P

MESH = pl.DeviceIdType.MESH
AXES = ("gy", "gz")
BF = jnp.bfloat16
F32 = jnp.float32
VMEM_LIMIT = 56 * 2**20
VM = pl.BlockSpec(memory_space=pltpu.VMEM)


def trig(length):
    index = np.arange(length, dtype=np.int64)
    angle = (index[:, None] * index[None, :] % length).astype(np.float64) * (2.0 * math.pi / length)
    factor = 1.0 / math.sqrt(length)
    return np.cos(angle) * factor, np.sin(angle) * factor


def as_bf16(array):
    return np.asarray(array, dtype=np.float32).astype(jnp.bfloat16)


def inverse_y_table(gy, rows):
    length = gy * rows
    cos, sin = trig(length)
    cos, sin = cos.reshape(gy, rows, length), sin.reshape(gy, rows, length)
    table = np.stack([np.stack([cos, sin], 2), np.stack([-sin, cos], 2)], 1)
    return as_bf16(table.reshape(2 * length, 2 * length))


def forward_y_table(gy, rows):
    length = gy * rows
    cos, sin = trig(length)
    cos, sin = cos.reshape(length, gy, rows), sin.reshape(length, gy, rows)
    table = np.stack([np.stack([cos, -sin], 2), np.stack([sin, cos], 2)], 0)
    return as_bf16(table.reshape(2 * length, 2 * length))


def z_table(length, inverse):
    cos, sin = trig(length)
    if inverse:
        table = np.block([[cos, -sin], [sin, cos]])
    else:
        table = np.block([[cos, sin], [-sin, cos]])
    return as_bf16(table)


def band_masks():
    zo, dz, j, zi = np.ogrid[0:8, 0:3, 0:3, 0:8]
    return (8 * (j - 1) + zi == zo + dz - 1).astype(np.float32)


def band_spread():
    hit = band_masks()
    eye = np.eye(18, dtype=np.float32)
    spread = np.einsum("odjz,kl->odkjlz", hit, eye)
    return as_bf16(spread.reshape(8, 54, 432))


def band_keep():
    hit = band_masks()
    keep = np.broadcast_to(hit.transpose(1, 0, 2, 3)[:, :, :, None, :], (3, 8, 3, 18, 8))
    return np.ascontiguousarray(keep.reshape(3, 8, 432)).astype(np.float32)


def band_spread_flipped():
    spread = band_spread().reshape(8, 3, 3, 3, 2, 432)
    return np.ascontiguousarray(spread[:, ::-1, ::-1, ::-1].reshape(8, 54, 432))


def band_gather():
    eye = np.eye(18, dtype=np.float32)
    both = np.stack([eye, eye.reshape(18, 3, 3, 2)[:, ::-1, ::-1].reshape(18, 18)])
    both = np.broadcast_to(both[:, None, :, None, :], (2, 3, 18, 8, 18))
    return np.ascontiguousarray(both.reshape(2, 432, 18))


def out_spread():
    q, dz, zo = np.ogrid[0:10, 0:3, 0:8]
    hit = (q == zo + dz).astype(np.float32)
    three, two = np.eye(3, dtype=np.float32), np.eye(2, dtype=np.float32)
    spread = np.einsum("qdz,yY,xX,oO->qdyxoXOYz", hit, three, three, two)
    return as_bf16(spread.reshape(10, 54, 144))


AHEAD = 24
ROWS = 4
COILS = 2
BESIDE = 16
AFTER_IMAGE = AHEAD + 4 * ROWS + 8 * COILS
CONV = 2
BACK = 4


def shifted(value, dy):
    if dy == 1:
        return value
    lane = lax.broadcasted_iota(jnp.int32, value.shape, value.ndim - 1)
    if dy == 0:
        return jnp.where(lane == 0, 0.0, pltpu.roll(value, 1, value.ndim - 1))
    return jnp.where(lane == 511, 0.0, pltpu.roll(value, 511, value.ndim - 1))


def fill_columns(images, cols):
    cols[pl.ds(0, 144), :] = jnp.zeros((144, 512), BF)
    cols[pl.ds(1296, 144), :] = jnp.zeros((144, 512), BF)
    for dx, image in enumerate(images):
        parts = [image(i) for i in range(2)]
        for dy in range(3):
            pair = jnp.stack([shifted(part, dy).reshape(8, 8, 512) for part in parts], axis=1)
            pair = pair.reshape(8, 16, 512).astype(BF)
            for zb in range(8):
                cols[pl.ds((zb + 1) * 144 + (dy * 3 + dx) * 16, 16), :] = pair[zb]


def gather_terms(total, keep, gather, order):
    pieces = []
    total = total.reshape(8, 32, 432)
    for dz in order:
        kept = total[0] * keep[dz, 0:1, :]
        for zo in range(1, 8):
            kept = kept + total[zo] * keep[dz, zo : zo + 1, :]
        pieces.append(
            jnp.dot(kept, gather, preferred_element_type=F32, precision=lax.Precision.HIGHEST)
        )
    return pieces


def cascade(
    norm,
    k_hbm, g_hbm, s_hbm, iy_hbm, fy_hbm, spread_in_hbm, spread_back_hbm, spread_out_hbm,
    iz, fz, mask, step, taps_in, bias, taps_out, keep, gather,
    out_hbm, weight, grad_in, grad_bias, grad_out,
    kv, gv, sens, iy, fy, stage, sk, sg, sf, rk, rg, rf,
    own_k, own_g, near_k, near_g, q_mid, q_send, q_near,
    cols, cols_g, hidden, slope, sum_in, sum_out, sum_b, first, second,
    flat, bias_cols, w_in, w_back, w_out, spread_in, spread_back, spread_out,
    load_sem, send_sem, recv_sem, store_sem,
):
    my_y, my_z = lax.axis_index("gy"), lax.axis_index("gz")
    me = my_y * 16 + my_z
    pos_x, pos_y, pos_z, pos_c = my_y % 4, my_y // 4 * 2 + my_z // 8, my_z // 2 % 4, my_z % 2
    left, right = (me + 127) % 128, (me + 1) % 128

    def pair(t):
        return (lax.div(t, 16), lax.rem(t, 16))

    loads = [
        pltpu.make_async_copy(src, dst, load_sem.at[n])
        for n, (src, dst) in enumerate(
            [(k_hbm, kv), (g_hbm, gv), (iy_hbm, iy), (s_hbm, sens), (fy_hbm, fy),
             (spread_in_hbm, spread_in), (spread_back_hbm, spread_back), (spread_out_hbm, spread_out)]
        )
    ]
    for load in loads:
        load.start()
    barrier = pltpu.get_barrier_semaphore()

    def greet(n, carry):
        pl.semaphore_signal(barrier, inc=1, device_id=pair(lax.rem(me + n, 128)), device_id_type=MESH)
        return carry

    lax.fori_loop(1, 128, greet, 0)

    def remote(src, dst, n, t):
        return pltpu.make_async_remote_copy(
            src_ref=src,
            dst_ref=dst,
            send_sem=send_sem.at[n],
            recv_sem=recv_sem.at[n],
            device_id=pair(t),
            device_id_type=MESH,
        )

    def target(i):
        n = lax.rem(i * 45, 128)
        x = lax.rem(pos_x + lax.rem(lax.div(n, 2), 4), 4)
        y = lax.rem(pos_y + lax.rem(lax.div(n, 8), 4), 4)
        z = lax.rem(pos_z + lax.div(n, 32), 4)
        c = lax.rem(pos_c + lax.rem(n, 2), 2)
        return (lax.div(y, 2) * 4 + x) * 16 + lax.rem(y, 2) * 8 + z * 2 + c

    def turn(source, index):
        depth, coil = index // 16, index % 16
        both = jnp.concatenate([source[0, coil, depth], source[1, coil, depth]], axis=0)
        stage[pl.ds(index, 128, stride=64), :] = both.T.astype(F32)

    def block_of(t):
        return stage[pl.ds(pl.multiple_of(t * 64, 64), 64), :].astype(BF)

    def turn_k(index, carry):
        turn(kv, index)
        return carry

    def half_of(t, half):
        return stage[pl.ds(pl.multiple_of(t * 64 + half * 32, 32), 32), :].astype(BF)

    loads[0].wait()
    for half in range(2):
        rows = pl.ds(half * 32, 32)

        def send_k(i, carry):
            t = target(i)
            sk[t, rows] = half_of(t, half)
            remote(sk.at[t, rows], rk.at[me, rows], 0, t).start()
            return carry

        lax.fori_loop(half * 32, half * 32 + 32, turn_k, 0, unroll=2)
        if half == 0:
            pl.semaphore_wait(barrier, 127)
        rk[me, rows] = half_of(me, half)
        lax.fori_loop(1, 128, send_k, 0)

    def turn_g(index, carry):
        turn(gv, index)
        return carry

    def keep_g(i, carry):
        sg[i] = block_of(i)
        return carry

    def later_g(i, carry):
        t = target(i)
        remote(sg.at[t], rg.at[me], 1, t).start()
        return carry

    loads[1].wait()
    lax.fori_loop(0, 64, turn_g, 0, unroll=2)
    rg[me] = block_of(me)
    lax.fori_loop(0, 128, keep_g, 0, unroll=4)
    lax.fori_loop(1, AHEAD, later_g, 0)

    for n in (5, 6, 7):
        loads[n].wait()
    contract = (((0,), (0,)), ((), ()))
    for tap in range(27):
        flat[0, pl.ds(tap * 2, 2), :] = taps_in[tap].astype(F32)
        flat[1, pl.ds(tap * 2, 2), :] = taps_out[tap].astype(F32)
    flat_in, flat_out = flat[0].astype(BF), flat[1].astype(BF)
    for zo in range(8):
        rows = pl.ds(zo * 32, 32)
        band = lax.dot_general(flat_in, spread_in[zo], contract, preferred_element_type=F32)
        w_in[rows, :] = band.astype(BF)
        band = lax.dot_general(flat_out, spread_back[zo], contract, preferred_element_type=F32)
        w_back[rows, :] = band.astype(BF)
    bands = [
        lax.dot_general(spread_out[q], flat_out, contract, preferred_element_type=F32)
        for q in range(10)
    ]
    w_out[...] = jnp.concatenate(bands, axis=1).astype(BF)

    def upright(row):
        return jnp.broadcast_to(row, (128, 128)).T

    bias_rows = upright(jnp.concatenate([bias[...]] * 4, axis=1))[:32]
    for zo in range(8):
        bias_cols[pl.ds(zo * 32, 32), :] = bias_rows
    for depth in range(4):
        row = mask[pl.ds(depth, 1), :].astype(F32) * step[...]
        weight[depth] = upright(jnp.concatenate([row, row], axis=1))[:64]

    def wait_blocks(sent, got, n):
        every = pltpu.make_async_remote_copy(
            src_ref=sent.at[pl.ds(0, 127)],
            dst_ref=got.at[pl.ds(0, 127)],
            send_sem=send_sem.at[n],
            recv_sem=recv_sem.at[n],
            device_id=pair(right),
            device_id_type=MESH,
        )
        every.wait_send()
        every.wait_recv()

    def both_ways(up, down, near, n):
        return [remote(up, near.at[0], n, right), remote(down, near.at[1], n + 1, left)]

    def to_image(tiles, image, near, n, push):
        def rows(m, carry):
            for i in range(ROWS):
                push(AHEAD + m * ROWS + i, 0)
            lines = jnp.concatenate(
                [tiles[pl.ds(gy * 16 + m * 4, 4)].reshape(256, 128) for gy in range(8)], axis=1
            )
            done = jnp.dot(lines, iy[...], preferred_element_type=F32)
            for lt in range(8):
                span = pl.ds(pl.multiple_of(lt * 1024 + m * 256, 256), 256)
                stage[span, :] = done[:, lt * 128 : lt * 128 + 128]
            return carry

        lax.fori_loop(0, 4, rows, 0)

        for chunk in range(4):
            lane = pl.ds(chunk * 128, 128)

            def coils(step_c, carry):
                real, imag = carry
                if chunk < COILS:
                    push(AHEAD + 4 * ROWS + chunk * 8 + step_c, 0)
                lines = []
                for c in (2 * step_c, 2 * step_c + 1):
                    halves = [
                        stage[pl.ds((p * 4 + chunk) * 1024 + c, 64, stride=16), :] for p in range(2)
                    ]
                    lines.append(jnp.concatenate(halves, axis=0).astype(BF))
                done = jnp.dot(
                    iz[...], jnp.concatenate(lines, axis=1), preferred_element_type=F32
                )
                for k in range(2):
                    c = 2 * step_c + k
                    c_r, c_i = done[:64, k * 128 : k * 128 + 128], done[64:, k * 128 : k * 128 + 128]
                    s_r, s_i = sens[0, 0, c, :, lane].astype(F32), sens[1, 0, c, :, lane].astype(F32)
                    real = real + (s_r * c_r + s_i * c_i)
                    imag = imag + (s_r * c_i - s_i * c_r)
                return real, imag

            zero = jnp.zeros((64, 128), F32)
            real, imag = lax.fori_loop(0, 8, coils, (zero, zero), unroll=2)
            image[chunk, 0] = real.astype(BF)
            image[chunk, 1] = imag.astype(BF)
            remote(image.at[chunk], near.at[0, chunk], n, right).start()
            remote(image.at[chunk], near.at[1, chunk], n + 1, left).start()
        return both_ways(image, image, near, n)

    def inside(side, value):
        return jnp.where(me > 0 if side == 0 else me < 127, value, 0.0)

    def plane(image, i):
        return jnp.concatenate([image[chunk, i] for chunk in range(4)], axis=1).astype(F32)

    def three(own, near):
        return (
            lambda i: inside(0, plane(near.at[0], i)),
            lambda i: plane(own, i),
            lambda i: inside(1, plane(near.at[1], i)),
        )

    loads[2].wait()
    loads[3].wait()
    wait_blocks(sk, rk, 0)
    copies = to_image(rk, own_k, near_k, 3, later_g)
    lax.fori_loop(AFTER_IMAGE, AFTER_IMAGE + BESIDE, later_g, 0)
    for copy in copies:
        copy.wait()

    fill_columns(three(own_k, near_k), cols)
    hidden[pl.ds(0, 32), :] = jnp.zeros((32, 512), BF)
    hidden[pl.ds(65 * 32, 32), :] = jnp.zeros((32, 512), BF)

    def conv_in_block(zb, carry):
        for i in range(CONV):
            later_g(AFTER_IMAGE + BESIDE + zb * CONV + i, 0)
        window = cols[pl.ds(pl.multiple_of(zb * 144, 16), 432), :]
        pre = jnp.dot(w_in[...], window, preferred_element_type=F32)
        pre = pre + jnp.concatenate([bias_cols[...]] * 4, axis=1)
        sig = jax.nn.sigmoid(pre)
        hidden[pl.ds(pl.multiple_of(zb * 256 + 32, 32), 256), :] = (pre * sig).astype(BF)
        slope[pl.ds(pl.multiple_of(zb * 256, 256), 256), :] = sig * (1.0 + pre * (1.0 - sig))
        return carry

    lax.fori_loop(0, 8, conv_in_block, 0)

    def conv_out_block(zb, carry):
        for i in range(CONV):
            later_g(AFTER_IMAGE + BESIDE + 8 * CONV + zb * CONV + i, 0)
        window = hidden[pl.ds(pl.multiple_of(zb * 256, 256), 320), :]
        terms = jnp.dot(w_out[...], window, preferred_element_type=F32).reshape(18, 8, 512)
        rows = pl.ds(pl.multiple_of(zb * 8, 8), 8)
        for dx in range(3):
            for o in range(2):
                base = (dx * 2 + o) * 3
                total = shifted(terms[base], 0) + terms[base + 1] + shifted(terms[base + 2], 2)
                q_mid[dx, o, rows, :] = total
        return carry

    for piece in range(4):
        lax.fori_loop(piece * 2, piece * 2 + 2, conv_out_block, 0)
        rows = pl.ds(piece * 16, 16)
        q_send[0, piece] = q_mid[0, :, rows, :].astype(BF)
        q_send[1, piece] = q_mid[2, :, rows, :].astype(BF)
        remote(q_send.at[0, piece], q_near.at[0, piece], 5, right).start()
        remote(q_send.at[1, piece], q_near.at[1, piece], 6, left).start()
    lax.fori_loop(AFTER_IMAGE + BESIDE + 16 * CONV, 128, later_g, 0)
    for copy in both_ways(q_send.at[0], q_send.at[1], q_near, 5):
        copy.wait()

    for piece in range(4):
        rows = pl.ds(piece * 16, 16)
        for o in range(2):
            total = inside(0, q_near[0, piece, o].astype(F32)) + q_mid[1, o, rows, :]
            total = total + inside(1, q_near[1, piece, o].astype(F32))
            q_mid[0, o, rows, :] = total.astype(BF).astype(F32)
    for chunk in range(4):
        lane = pl.ds(chunk * 128, 128)
        r_r, r_i = q_mid[0, 0, :, lane], q_mid[0, 1, :, lane]

        def spread(step_c, carry):
            lines = []
            for c in (2 * step_c, 2 * step_c + 1):
                s_r, s_i = sens[0, 0, c, :, lane].astype(F32), sens[1, 0, c, :, lane].astype(F32)
                both = [s_r * r_r - s_i * r_i, s_r * r_i + s_i * r_r]
                lines.append(jnp.concatenate(both, axis=0).astype(BF))
            done = jnp.dot(fz[...], jnp.concatenate(lines, axis=1), preferred_element_type=F32)
            for k in range(2):
                for p in range(2):
                    rows = pl.ds((p * 4 + chunk) * 1024 + 2 * step_c + k, 64, stride=16)
                    stage[rows, :] = done[p * 64 : p * 64 + 64, k * 128 : k * 128 + 128]
            return carry

        lax.fori_loop(0, 8, spread, 0, unroll=2)
    loads[4].wait()

    def send_f(m, carry):
        lines = [stage[pl.ds(pl.multiple_of(lt * 1024 + m * 256, 256), 256), :] for lt in range(8)]
        lines = jnp.concatenate([part.astype(BF) for part in lines], axis=1)
        done = jnp.dot(lines, fy[...], preferred_element_type=F32).astype(BF)
        for gy in range(8):
            sf[pl.ds(gy * 16 + m * 4, 4)] = done[:, gy * 128 : gy * 128 + 128].reshape(4, 64, 128)

        return carry

    def start_f(i, carry):
        t = target(i)
        remote(sf.at[t], rf.at[me], 2, t).start()
        return carry

    lax.fori_loop(0, 4, send_f, 0)
    rf[me] = sf[me]
    lax.fori_loop(1, AHEAD, start_f, 0)

    wait_blocks(sg, rg, 1)
    copies = to_image(rg, own_g, near_g, 7, start_f)
    lax.fori_loop(AFTER_IMAGE, AFTER_IMAGE + BESIDE, start_f, 0)
    for copy in copies:
        copy.wait()
    fill_columns(three(own_g, near_g), cols_g)
    sum_in[...] = jnp.zeros_like(sum_in)
    sum_out[...] = jnp.zeros_like(sum_out)
    sum_b[...] = jnp.zeros_like(sum_b)
    nt = (((1,), (1,)), ((), ()))

    def back_block(zb, carry):
        for i in range(BACK):
            start_f(AFTER_IMAGE + BESIDE + zb * BACK + i, 0)
        span = pl.ds(pl.multiple_of(zb * 144, 16), 432)
        window_g = cols_g[span, :]
        back = jnp.dot(w_back[...], window_g, preferred_element_type=F32)
        back = (back * slope[pl.ds(pl.multiple_of(zb * 256, 256), 256), :]).astype(BF)
        sum_in[...] += lax.dot_general(back, cols[span, :], nt, preferred_element_type=F32)
        held = hidden[pl.ds(pl.multiple_of(zb * 256 + 32, 32), 256), :]
        sum_out[...] += lax.dot_general(held, window_g, nt, preferred_element_type=F32)
        wide = back.astype(F32)
        sum_b[...] += wide[:, :128] + wide[:, 128:256] + wide[:, 256:384] + wide[:, 384:]
        return carry

    lax.fori_loop(0, 8, back_block, 0)
    lax.fori_loop(AFTER_IMAGE + BESIDE + 8 * BACK, 128, start_f, 0)
    bias_sum = jnp.sum(sum_b[...].reshape(8, 32, 128), axis=0)
    bias_sum = jnp.sum(bias_sum, axis=1, keepdims=True)
    pieces = gather_terms(sum_in[...], keep, gather[0], (0, 1, 2))
    pieces += gather_terms(sum_out[...], keep, gather[1], (2, 1, 0))
    pieces.append(jnp.broadcast_to(bias_sum, (32, 20)))

    def share(buffer, mine, count, n, device):
        def start(step, carry):
            remote(buffer.at[mine], buffer.at[mine], n, device((mine + step) % count)).start()
            return carry

        lax.fori_loop(1, count, start, 0)

    def collect(buffer, count, n):
        every = pltpu.make_async_remote_copy(
            src_ref=buffer.at[pl.ds(0, count - 1)],
            dst_ref=buffer.at[pl.ds(0, count - 1)],
            send_sem=send_sem.at[n],
            recv_sem=recv_sem.at[n],
            device_id=pair(right),
            device_id_type=MESH,
        )
        every.wait_send()
        every.wait_recv()
        total = buffer[0]
        for index in range(1, count):
            total = total + buffer[index]
        return total

    first[my_z] = jnp.concatenate(pieces, axis=1)
    share(first, my_z, 16, 9, lambda to: my_y * 16 + to)

    wait_blocks(sf, rf, 2)

    def widen(x, carry):
        stage[pl.ds(pl.multiple_of(x * 64, 64), 64), :] = rf[x].astype(F32)
        return carry

    lax.fori_loop(0, 128, widen, 0, unroll=4)
    def finish(index, carry):
        depth, coil = lax.div(index, 16), lax.rem(index, 16)
        both = stage[pl.ds(index, 128, stride=64), :].astype(BF).T
        kv[0, coil, depth], kv[1, coil, depth] = both[:64], both[64:]
        return carry

    stores = []
    for depth in range(4):
        if depth == 2:
            second[my_y] = collect(first, 16, 9)
            share(second, my_y, 8, 10, lambda to: to * 16 + my_z)
        lax.fori_loop(depth * 16, depth * 16 + 16, finish, 0, unroll=2)
        stores.append(
            pltpu.make_async_copy(kv.at[:, :, depth], out_hbm.at[:, :, depth], store_sem.at[depth])
        )
        stores[-1].start()
    total = jnp.concatenate([collect(second, 8, 10) * norm] * 4, axis=0).T[:, :32]
    for tap in range(27):
        grad_in[tap] = total[tap * 2 : tap * 2 + 2]
        grad_out[tap] = total[54 + tap * 2 : 56 + tap * 2]
    grad_bias[...] = total[108:109]
    for store in stores:
        store.wait()


def run_cascade(norm, *operands):
    blocks = pltpu.VMEM((128, 64, 128), BF)
    tile = pltpu.VMEM((2, 16, 4, 64, 128), BF)
    image = pltpu.VMEM((4, 2, 64, 128), BF)
    near = pltpu.VMEM((2, 4, 2, 64, 128), BF)
    pieces = pltpu.VMEM((2, 4, 2, 16, 512), BF)
    table = pltpu.VMEM((1024, 1024), BF)
    hbm = pl.BlockSpec(memory_space=pl.ANY)
    return pl.pallas_call(
        functools.partial(cascade, norm),
        out_shape=(
            jax.ShapeDtypeStruct((2, 16, 4, 64, 128), BF),
            jax.ShapeDtypeStruct((4, 64, 128), F32),
            jax.ShapeDtypeStruct((27, 2, 32), F32),
            jax.ShapeDtypeStruct((1, 32), F32),
            jax.ShapeDtypeStruct((27, 2, 32), F32),
        ),
        in_specs=[hbm] * 8 + [VM] * 9,
        out_specs=(hbm, VM, VM, VM, VM),
        scratch_shapes=[
            tile, tile,
            pltpu.VMEM((2, 1, 16, 64, 512), BF),
            table, table,
            pltpu.VMEM((8192, 128), F32),
            blocks, blocks, blocks, blocks, blocks, blocks,
            image, image, near, near,
            pltpu.VMEM((3, 2, 64, 512), F32),
            pieces, pieces,
            pltpu.VMEM((1440, 512), BF),
            pltpu.VMEM((1440, 512), BF),
            pltpu.VMEM((66 * 32, 512), BF),
            pltpu.VMEM((2048, 512), F32),
            pltpu.VMEM((256, 432), F32),
            pltpu.VMEM((256, 432), F32),
            pltpu.VMEM((256, 128), F32),
            pltpu.VMEM((16, 32, 128), F32),
            pltpu.VMEM((8, 32, 128), F32),
            pltpu.VMEM((2, 54, 32), F32),
            pltpu.VMEM((256, 128), F32),
            pltpu.VMEM((256, 432), BF),
            pltpu.VMEM((256, 432), BF),
            pltpu.VMEM((144, 320), BF),
            pltpu.VMEM((8, 54, 432), BF),
            pltpu.VMEM((8, 54, 432), BF),
            pltpu.VMEM((10, 54, 144), BF),
            pltpu.SemaphoreType.DMA((8,)),
            pltpu.SemaphoreType.DMA((11,)),
            pltpu.SemaphoreType.DMA((11,)),
            pltpu.SemaphoreType.DMA((4,)),
        ],
        compiler_params=pltpu.CompilerParams(
            collective_id=0, has_side_effects=True, vmem_limit_bytes=VMEM_LIMIT
        ),
        name="cascade",
    )(*operands)


def on_device(
    kspace, measured, sample_mask, step_size, coil_field, conv_in, bias_in, conv_out, cotangent
):
    count_y, count_z = lax.axis_size("gy"), lax.axis_size("gz")
    row_tile, x_cells, depth_tile = kspace.shape[3], kspace.shape[4], kspace.shape[2]
    inverse_y = jnp.asarray(inverse_y_table(count_y, row_tile))
    forward_y = jnp.asarray(forward_y_table(count_y, row_tile))
    inverse_z = jnp.asarray(z_table(count_z * depth_tile, True))
    forward_z = jnp.asarray(z_table(count_z * depth_tile, False))
    norm = 1.0 / math.sqrt(x_cells * row_tile * count_y * depth_tile * count_z)
    refine, weight, grad_in, grad_bias, grad_out = run_cascade(
        norm, kspace, cotangent, coil_field, inverse_y, forward_y,
        jnp.asarray(band_spread()), jnp.asarray(band_spread_flipped()), jnp.asarray(out_spread()),
        inverse_z, forward_z, sample_mask, step_size.reshape(1, 1),
        conv_in.transpose(2, 3, 4, 1, 0).reshape(27, 2, 32), bias_in.reshape(1, 32),
        conv_out.transpose(2, 3, 4, 0, 1).reshape(27, 2, 32),
        jnp.asarray(band_keep()), jnp.asarray(band_gather()),
    )
    current = kspace.astype(F32)
    kspace_next = current - weight * (current - measured.astype(F32)) + refine.astype(F32)
    kspace_next = kspace_next.astype(BF)
    grad_in = grad_in.reshape(3, 3, 3, 2, 32).transpose(4, 3, 0, 1, 2)
    grad_out = grad_out.reshape(3, 3, 3, 2, 32).transpose(3, 4, 0, 1, 2)
    return kspace_next, grad_in, grad_bias.reshape(32), grad_out


def solution(mesh):
    tile = P(None, None, "gz", "gy", None)
    in_specs = (
        tile,
        tile,
        P("gz", "gy"),
        P(),
        P(None, AXES, None, None, None),
        P(),
        P(),
        P(),
        tile,
    )
    out_specs = (tile, P(), P(), P())
    return jax.shard_map(
        on_device, mesh=mesh, in_specs=in_specs, out_specs=out_specs, check_vma=False
    )
```

```python
import functools
import math

import jax
import jax.numpy as jnp
import numpy as np
from jax import lax
from jax.experimental import pallas as pl
from jax.experimental.pallas import tpu as pltpu
from jax.sharding import PartitionSpec as P

MESH = pl.DeviceIdType.MESH
AXES = ("gy", "gz")
BF = jnp.bfloat16
F32 = jnp.float32
VMEM_LIMIT = 56 * 2**20
VM = pl.BlockSpec(memory_space=pltpu.VMEM)


def trig(length):
    index = np.arange(length, dtype=np.int64)
    angle = (index[:, None] * index[None, :] % length).astype(np.float64) * (2.0 * math.pi / length)
    factor = 1.0 / math.sqrt(length)
    return np.cos(angle) * factor, np.sin(angle) * factor


def as_bf16(array):
    return np.asarray(array, dtype=np.float32).astype(jnp.bfloat16)


def inverse_y_table(gy, rows):
    length = gy * rows
    cos, sin = trig(length)
    cos, sin = cos.reshape(gy, rows, length), sin.reshape(gy, rows, length)
    table = np.stack([np.stack([cos, sin], 2), np.stack([-sin, cos], 2)], 1)
    return as_bf16(table.reshape(2 * length, 2 * length))


def forward_y_table(gy, rows):
    length = gy * rows
    cos, sin = trig(length)
    cos, sin = cos.reshape(length, gy, rows), sin.reshape(length, gy, rows)
    table = np.stack([np.stack([cos, -sin], 2), np.stack([sin, cos], 2)], 0)
    return as_bf16(table.reshape(2 * length, 2 * length))


def z_table(length, inverse):
    cos, sin = trig(length)
    if inverse:
        table = np.block([[cos, -sin], [sin, cos]])
    else:
        table = np.block([[cos, sin], [-sin, cos]])
    return as_bf16(table)


def band_masks():
    zo, dz, j, zi = np.ogrid[0:8, 0:3, 0:3, 0:8]
    return (8 * (j - 1) + zi == zo + dz - 1).astype(np.float32)


def band_spread():
    hit = band_masks()
    eye = np.eye(18, dtype=np.float32)
    spread = np.einsum("odjz,kl->odkjlz", hit, eye)
    return as_bf16(spread.reshape(8, 54, 432))


def band_keep():
    hit = band_masks()
    keep = np.broadcast_to(hit.transpose(1, 0, 2, 3)[:, :, :, None, :], (3, 8, 3, 18, 8))
    return np.ascontiguousarray(keep.reshape(3, 8, 432)).astype(np.float32)


def band_spread_flipped():
    spread = band_spread().reshape(8, 3, 3, 3, 2, 432)
    return np.ascontiguousarray(spread[:, ::-1, ::-1, ::-1].reshape(8, 54, 432))


def band_gather():
    eye = np.eye(18, dtype=np.float32)
    both = np.stack([eye, eye.reshape(18, 3, 3, 2)[:, ::-1, ::-1].reshape(18, 18)])
    both = np.broadcast_to(both[:, None, :, None, :], (2, 3, 18, 8, 18))
    return np.ascontiguousarray(both.reshape(2, 432, 18))


def out_spread():
    q, dz, zo = np.ogrid[0:10, 0:3, 0:8]
    hit = (q == zo + dz).astype(np.float32)
    three, two = np.eye(3, dtype=np.float32), np.eye(2, dtype=np.float32)
    spread = np.einsum("qdz,yY,xX,oO->qdyxoXOYz", hit, three, three, two)
    return as_bf16(spread.reshape(10, 54, 144))


AHEAD = 24
ROWS = 4
COILS = 2
BESIDE = 16
AFTER_IMAGE = AHEAD + ROWS + 8 * COILS
CONV = 2
BACK = 4


def shifted(value, dy):
    if dy == 1:
        return value
    lane = lax.broadcasted_iota(jnp.int32, value.shape, value.ndim - 1)
    if dy == 0:
        return jnp.where(lane == 0, 0.0, pltpu.roll(value, 1, value.ndim - 1))
    return jnp.where(lane == 511, 0.0, pltpu.roll(value, 511, value.ndim - 1))


def clear_columns(cols):
    cols[pl.ds(0, 144), :] = jnp.zeros((144, 512), BF)
    cols[pl.ds(1296, 144), :] = jnp.zeros((144, 512), BF)


def fill_columns(dx, image, cols):
    parts = [image(i) for i in range(2)]
    for dy in range(3):
        pair = jnp.stack([shifted(part, dy).reshape(8, 8, 512) for part in parts], axis=1)
        pair = pair.reshape(8, 16, 512).astype(BF)
        for zb in range(8):
            cols[pl.ds((zb + 1) * 144 + (dy * 3 + dx) * 16, 16), :] = pair[zb]


def gather_terms(total, keep, gather, order):
    pieces = []
    total = total.reshape(8, 32, 432)
    for dz in order:
        kept = total[0] * keep[dz, 0:1, :]
        for zo in range(1, 8):
            kept = kept + total[zo] * keep[dz, zo : zo + 1, :]
        pieces.append(
            jnp.dot(kept, gather, preferred_element_type=F32, precision=lax.Precision.HIGHEST)
        )
    return pieces


def cascade(
    norm,
    k_hbm, g_hbm, s_hbm, iy_hbm, fy_hbm, spread_in_hbm, spread_back_hbm, spread_out_hbm,
    iz, fz, mask, step, taps_in, bias, taps_out, keep, gather,
    out_hbm, weight, grad_in, grad_bias, grad_out,
    kv, gv, sens, iy, fy, stage, sk, sg, sf, rk, rg, rf,
    own_k, own_g, near_k, near_g, q_mid, q_send, q_near,
    cols, cols_g, hidden, slope, sum_in, sum_out, sum_b, first, second,
    flat, bias_cols, w_in, w_back, w_out, spread_in, spread_back, spread_out,
    load_sem, send_sem, recv_sem, store_sem,
):
    my_y, my_z = lax.axis_index("gy"), lax.axis_index("gz")
    me = my_y * 16 + my_z
    pos_x, pos_y, pos_z, pos_c = my_y % 4, my_y // 4 * 2 + my_z // 8, my_z // 2 % 4, my_z % 2
    left, right = (me + 127) % 128, (me + 1) % 128

    def pair(t):
        return (lax.div(t, 16), lax.rem(t, 16))

    loads = [
        pltpu.make_async_copy(src, dst, load_sem.at[n])
        for n, (src, dst) in enumerate(
            [(k_hbm, kv), (g_hbm, gv), (iy_hbm, iy), (s_hbm, sens), (fy_hbm, fy),
             (spread_in_hbm, spread_in), (spread_back_hbm, spread_back), (spread_out_hbm, spread_out)]
        )
    ]
    for load in loads:
        load.start()
    barrier = pltpu.get_barrier_semaphore()

    def greet(n, carry):
        pl.semaphore_signal(barrier, inc=1, device_id=pair(lax.rem(me + n, 128)), device_id_type=MESH)
        return carry

    lax.fori_loop(1, 128, greet, 0)

    def remote(src, dst, n, t):
        return pltpu.make_async_remote_copy(
            src_ref=src,
            dst_ref=dst,
            send_sem=send_sem.at[n],
            recv_sem=recv_sem.at[n],
            device_id=pair(t),
            device_id_type=MESH,
        )

    def target(i):
        n = lax.rem(i * 45, 128)
        x = lax.rem(pos_x + lax.rem(lax.div(n, 2), 4), 4)
        y = lax.rem(pos_y + lax.rem(lax.div(n, 8), 4), 4)
        z = lax.rem(pos_z + lax.div(n, 32), 4)
        c = lax.rem(pos_c + lax.rem(n, 2), 2)
        return (lax.div(y, 2) * 4 + x) * 16 + lax.rem(y, 2) * 8 + z * 2 + c

    nt = (((1,), (1,)), ((), ()))

    def turn(source, index):
        depth, coil = index // 16, index % 16
        both = jnp.concatenate([source[0, coil, depth], source[1, coil, depth]], axis=0)
        stage[pl.ds(index, 128, stride=64), :] = both.T.astype(F32)

    def block_of(t):
        return stage[pl.ds(pl.multiple_of(t * 64, 64), 64), :].astype(BF)

    def turn_k(index, carry):
        turn(kv, index)
        return carry

    def half_of(t, half):
        return stage[pl.ds(pl.multiple_of(t * 64 + half * 32, 32), 32), :].astype(BF)

    loads[0].wait()
    for half in range(2):
        rows = pl.ds(half * 32, 32)

        def send_k(i, carry):
            t = target(i)
            sk[t, rows] = half_of(t, half)
            remote(sk.at[t, rows], rk.at[me, rows], 11 * half, t).start()
            return carry

        lax.fori_loop(half * 32, half * 32 + 32, turn_k, 0, unroll=4)
        if half == 0:
            pl.semaphore_wait(barrier, 127)
        rk[me, rows] = half_of(me, half)
        lax.fori_loop(1, 128, send_k, 0)

    def turn_g(index, carry):
        turn(gv, index)
        return carry

    def keep_g(i, carry):
        sg[i] = block_of(i)
        return carry

    def later_g(i, carry):
        t = target(i)
        remote(sg.at[t], rg.at[me], 1, t).start()
        return carry

    loads[1].wait()
    lax.fori_loop(0, 64, turn_g, 0, unroll=4)
    rg[me] = block_of(me)
    lax.fori_loop(0, 128, keep_g, 0, unroll=4)
    lax.fori_loop(1, AHEAD, later_g, 0)

    for n in (5, 6, 7):
        loads[n].wait()
    contract = (((0,), (0,)), ((), ()))
    for tap in range(27):
        flat[0, pl.ds(tap * 2, 2), :] = taps_in[tap].astype(F32)
        flat[1, pl.ds(tap * 2, 2), :] = taps_out[tap].astype(F32)
    flat_in, flat_out = flat[0].astype(BF), flat[1].astype(BF)
    for zo in range(8):
        rows = pl.ds(zo * 32, 32)
        band = lax.dot_general(flat_in, spread_in[zo], contract, preferred_element_type=F32)
        w_in[rows, :] = band.astype(BF)
        band = lax.dot_general(flat_out, spread_back[zo], contract, preferred_element_type=F32)
        w_back[rows, :] = band.astype(BF)
    bands = [
        lax.dot_general(spread_out[q], flat_out, contract, preferred_element_type=F32)
        for q in range(10)
    ]
    w_out[...] = jnp.concatenate(bands, axis=1).astype(BF)

    def upright(row):
        return jnp.broadcast_to(row, (128, 128)).T

    bias_rows = upright(jnp.concatenate([bias[...]] * 4, axis=1))[:32]
    for zo in range(8):
        bias_cols[pl.ds(zo * 32, 32), :] = bias_rows
    for depth in range(4):
        row = mask[pl.ds(depth, 1), :].astype(F32) * step[...]
        weight[depth] = upright(jnp.concatenate([row, row], axis=1))[:64]

    def wait_blocks(sent, got, n, rows=64):
        every = pltpu.make_async_remote_copy(
            src_ref=sent.at[pl.ds(0, 127), pl.ds(0, rows)],
            dst_ref=got.at[pl.ds(0, 127), pl.ds(0, rows)],
            send_sem=send_sem.at[n],
            recv_sem=recv_sem.at[n],
            device_id=pair(right),
            device_id_type=MESH,
        )
        every.wait_send()
        every.wait_recv()

    def both_ways(up, down, near, n):
        return [remote(up, near.at[0], n, right), remote(down, near.at[1], n + 1, left)]

    def to_image(tiles, image, near, n, push, *arrivals):
        parts = len(arrivals)
        depth = 64 // parts

        for part, (sent, sem) in enumerate(arrivals):
            wait_blocks(sent, tiles, sem, depth)

            def rows(m, carry):
                push(AHEAD + 4 // parts * part + m, 0)
                lines = jnp.concatenate(
                    [
                        tiles[pl.ds(gy * 16 + m * 4 * parts, 4 * parts), pl.ds(part * depth, depth)]
                        .reshape(256, 128)
                        for gy in range(8)
                    ],
                    axis=1,
                )
                done = jnp.dot(lines, iy[...], preferred_element_type=F32)
                done = done.reshape(4 * parts, depth, 1024)
                for lt in range(8):
                    for k in range(4 * parts):
                        start = lt * 1024 + (m * 4 * parts + k) * 64 + part * depth
                        stage[pl.ds(pl.multiple_of(start, 32), depth), :] = done[
                            k, :, lt * 128 : lt * 128 + 128
                        ]
                return carry

            lax.fori_loop(0, 4 // parts, rows, 0)

        for chunk in range(4):
            lane = pl.ds(chunk * 128, 128)

            def coils(step_c, carry):
                real, imag = carry
                if chunk < COILS:
                    push(AHEAD + ROWS + chunk * 8 + step_c, 0)
                lines = []
                for c in (2 * step_c, 2 * step_c + 1):
                    halves = [
                        stage[pl.ds((p * 4 + chunk) * 1024 + c, 64, stride=16), :] for p in range(2)
                    ]
                    lines.append(jnp.concatenate(halves, axis=0).astype(BF))
                done = jnp.dot(
                    iz[...], jnp.concatenate(lines, axis=1), preferred_element_type=F32
                )
                for k in range(2):
                    c = 2 * step_c + k
                    c_r, c_i = done[:64, k * 128 : k * 128 + 128], done[64:, k * 128 : k * 128 + 128]
                    s_r, s_i = sens[0, 0, c, :, lane].astype(F32), sens[1, 0, c, :, lane].astype(F32)
                    real = real + (s_r * c_r + s_i * c_i)
                    imag = imag + (s_r * c_i - s_i * c_r)
                return real, imag

            zero = jnp.zeros((64, 128), F32)
            real, imag = lax.fori_loop(0, 8, coils, (zero, zero), unroll=2)
            image[chunk, 0] = real.astype(BF)
            image[chunk, 1] = imag.astype(BF)
            remote(image.at[chunk], near.at[0, chunk], n, right).start()
            remote(image.at[chunk], near.at[1, chunk], n + 1, left).start()
        return both_ways(image, image, near, n)

    def inside(side, value):
        return jnp.where(me > 0 if side == 0 else me < 127, value, 0.0)

    def plane(image, i):
        return jnp.concatenate([image[chunk, i] for chunk in range(4)], axis=1).astype(F32)

    def fill(own, near, copies, columns):
        fill_columns(1, lambda i: plane(own, i), columns)
        for side, copy in enumerate(copies):
            copy.wait()
            fill_columns(2 * side, lambda i: inside(side, plane(near.at[side], i)), columns)

    loads[2].wait()
    loads[3].wait()
    copies = to_image(rk, own_k, near_k, 3, later_g, (sk, 0), (sk, 11))
    lax.fori_loop(AFTER_IMAGE, AFTER_IMAGE + BESIDE, later_g, 0)
    clear_columns(cols)
    fill(own_k, near_k, copies, cols)
    hidden[pl.ds(0, 32), :] = jnp.zeros((32, 512), BF)
    hidden[pl.ds(65 * 32, 32), :] = jnp.zeros((32, 512), BF)

    def conv_in_block(zb, carry):
        for i in range(CONV):
            later_g(AFTER_IMAGE + BESIDE + zb * CONV + i, 0)
        window = cols[pl.ds(pl.multiple_of(zb * 144, 16), 432), :]
        pre = jnp.dot(w_in[...], window, preferred_element_type=F32)
        pre = pre + jnp.concatenate([bias_cols[...]] * 4, axis=1)
        sig = jax.nn.sigmoid(pre)
        hidden[pl.ds(pl.multiple_of(zb * 256 + 32, 32), 256), :] = (pre * sig).astype(BF)
        slope[pl.ds(pl.multiple_of(zb * 256, 256), 256), :] = sig * (1.0 + pre * (1.0 - sig))
        return carry

    lax.fori_loop(0, 8, conv_in_block, 0, unroll=2)

    def conv_out_block(zb, carry):
        for i in range(CONV):
            later_g(AFTER_IMAGE + BESIDE + 8 * CONV + zb * CONV + i, 0)
        window = hidden[pl.ds(pl.multiple_of(zb * 256, 256), 320), :]
        terms = jnp.dot(w_out[...], window, preferred_element_type=F32).reshape(18, 8, 512)
        rows = pl.ds(pl.multiple_of(zb * 8, 8), 8)
        for dx in range(3):
            for o in range(2):
                base = (dx * 2 + o) * 3
                total = shifted(terms[base], 0) + terms[base + 1] + shifted(terms[base + 2], 2)
                q_mid[dx, o, rows, :] = total
        return carry

    for piece in range(4):
        lax.fori_loop(piece * 2, piece * 2 + 2, conv_out_block, 0)
        rows = pl.ds(piece * 16, 16)
        q_send[0, piece] = q_mid[0, :, rows, :].astype(BF)
        q_send[1, piece] = q_mid[2, :, rows, :].astype(BF)
        remote(q_send.at[0, piece], q_near.at[0, piece], 5, right).start()
        remote(q_send.at[1, piece], q_near.at[1, piece], 6, left).start()
    lax.fori_loop(AFTER_IMAGE + BESIDE + 16 * CONV, 128, later_g, 0)
    for copy in both_ways(q_send.at[0], q_send.at[1], q_near, 5):
        copy.wait()

    for piece in range(4):
        rows = pl.ds(piece * 16, 16)
        for o in range(2):
            total = inside(0, q_near[0, piece, o].astype(F32)) + q_mid[1, o, rows, :]
            total = total + inside(1, q_near[1, piece, o].astype(F32))
            q_mid[0, o, rows, :] = total.astype(BF).astype(F32)
    for chunk in range(4):
        lane = pl.ds(chunk * 128, 128)
        r_r, r_i = q_mid[0, 0, :, lane], q_mid[0, 1, :, lane]

        def spread(step_c, carry):
            lines = []
            for c in (2 * step_c, 2 * step_c + 1):
                s_r, s_i = sens[0, 0, c, :, lane].astype(F32), sens[1, 0, c, :, lane].astype(F32)
                both = [s_r * r_r - s_i * r_i, s_r * r_i + s_i * r_r]
                lines.append(jnp.concatenate(both, axis=0).astype(BF))
            done = jnp.dot(fz[...], jnp.concatenate(lines, axis=1), preferred_element_type=F32)
            for k in range(2):
                for p in range(2):
                    rows = pl.ds((p * 4 + chunk) * 1024 + 2 * step_c + k, 64, stride=16)
                    stage[rows, :] = done[p * 64 : p * 64 + 64, k * 128 : k * 128 + 128]
            return carry

        lax.fori_loop(0, 8, spread, 0, unroll=2)
    loads[4].wait()

    def send_f(m, carry):
        lines = [stage[pl.ds(pl.multiple_of(lt * 1024 + m * 256, 256), 256), :] for lt in range(8)]
        lines = jnp.concatenate([part.astype(BF) for part in lines], axis=1)
        done = jnp.dot(lines, fy[...], preferred_element_type=F32).astype(BF)
        for gy in range(8):
            sf[pl.ds(gy * 16 + m * 4, 4)] = done[:, gy * 128 : gy * 128 + 128].reshape(4, 64, 128)

        return carry

    def start_f(i, carry):
        t = target(i)
        remote(sf.at[t], rf.at[me], 2, t).start()
        return carry

    lax.fori_loop(0, 4, send_f, 0)
    rf[me] = sf[me]
    lax.fori_loop(1, AHEAD, start_f, 0)

    copies = to_image(rg, own_g, near_g, 7, start_f, (sg, 1))
    lax.fori_loop(AFTER_IMAGE, AFTER_IMAGE + BESIDE, start_f, 0)
    clear_columns(cols_g)
    fill(own_g, near_g, copies, cols_g)
    sum_in[...] = jnp.zeros_like(sum_in)
    sum_out[...] = jnp.zeros_like(sum_out)
    sum_b[...] = jnp.zeros_like(sum_b)
    def back_block(zb, carry):
        for i in range(BACK):
            start_f(AFTER_IMAGE + BESIDE + zb * BACK + i, 0)
        span = pl.ds(pl.multiple_of(zb * 144, 16), 432)
        window_g = cols_g[span, :]
        back = jnp.dot(w_back[...], window_g, preferred_element_type=F32)
        back = (back * slope[pl.ds(pl.multiple_of(zb * 256, 256), 256), :]).astype(BF)
        sum_in[...] += lax.dot_general(back, cols[span, :], nt, preferred_element_type=F32)
        held = hidden[pl.ds(pl.multiple_of(zb * 256 + 32, 32), 256), :]
        sum_out[...] += lax.dot_general(held, window_g, nt, preferred_element_type=F32)
        wide = back.astype(F32)
        sum_b[...] += wide[:, :128] + wide[:, 128:256] + wide[:, 256:384] + wide[:, 384:]
        return carry

    lax.fori_loop(0, 8, back_block, 0, unroll=2)
    lax.fori_loop(AFTER_IMAGE + BESIDE + 8 * BACK, 128, start_f, 0)
    bias_sum = jnp.sum(sum_b[...].reshape(8, 32, 128), axis=0)
    bias_sum = jnp.sum(bias_sum, axis=1, keepdims=True)
    pieces = gather_terms(sum_in[...], keep, gather[0], (0, 1, 2))
    pieces += gather_terms(sum_out[...], keep, gather[1], (2, 1, 0))
    pieces.append(jnp.broadcast_to(bias_sum, (32, 20)))

    def share(buffer, mine, count, n, device):
        def start(step, carry):
            remote(buffer.at[mine], buffer.at[mine], n, device((mine + step) % count)).start()
            return carry

        lax.fori_loop(1, count, start, 0)

    def collect(buffer, count, n):
        every = pltpu.make_async_remote_copy(
            src_ref=buffer.at[pl.ds(0, count - 1)],
            dst_ref=buffer.at[pl.ds(0, count - 1)],
            send_sem=send_sem.at[n],
            recv_sem=recv_sem.at[n],
            device_id=pair(right),
            device_id_type=MESH,
        )
        every.wait_send()
        every.wait_recv()
        total = buffer[0]
        for index in range(1, count):
            total = total + buffer[index]
        return total

    first[my_z] = jnp.concatenate(pieces, axis=1)
    share(first, my_z, 16, 9, lambda to: my_y * 16 + to)

    wait_blocks(sf, rf, 2)

    second[my_y] = collect(first, 16, 9)
    share(second, my_y, 8, 10, lambda to: to * 16 + my_z)

    def widen(x, carry):
        stage[pl.ds(pl.multiple_of(x * 64, 64), 64), :] = rf[x].astype(F32)
        return carry

    lax.fori_loop(0, 128, widen, 0, unroll=4)
    def finish(index, carry):
        depth, coil = lax.div(index, 16), lax.rem(index, 16)
        both = stage[pl.ds(index, 128, stride=64), :].astype(BF).T
        kv[0, coil, depth], kv[1, coil, depth] = both[:64], both[64:]
        return carry

    stores = []
    for depth in range(4):
        lax.fori_loop(depth * 16, depth * 16 + 16, finish, 0, unroll=4)
        stores.append(
            pltpu.make_async_copy(kv.at[:, :, depth], out_hbm.at[:, :, depth], store_sem.at[depth])
        )
        stores[-1].start()
    total = jnp.concatenate([collect(second, 8, 10) * norm] * 4, axis=0).T[:, :32]
    for tap in range(27):
        grad_in[tap] = total[tap * 2 : tap * 2 + 2]
        grad_out[tap] = total[54 + tap * 2 : 56 + tap * 2]
    grad_bias[...] = total[108:109]
    for store in stores:
        store.wait()


def run_cascade(norm, *operands):
    blocks = pltpu.VMEM((128, 64, 128), BF)
    tile = pltpu.VMEM((2, 16, 4, 64, 128), BF)
    image = pltpu.VMEM((4, 2, 64, 128), BF)
    near = pltpu.VMEM((2, 4, 2, 64, 128), BF)
    pieces = pltpu.VMEM((2, 4, 2, 16, 512), BF)
    table = pltpu.VMEM((1024, 1024), BF)
    hbm = pl.BlockSpec(memory_space=pl.ANY)
    return pl.pallas_call(
        functools.partial(cascade, norm),
        out_shape=(
            jax.ShapeDtypeStruct((2, 16, 4, 64, 128), BF),
            jax.ShapeDtypeStruct((4, 64, 128), F32),
            jax.ShapeDtypeStruct((27, 2, 32), F32),
            jax.ShapeDtypeStruct((1, 32), F32),
            jax.ShapeDtypeStruct((27, 2, 32), F32),
        ),
        in_specs=[hbm] * 8 + [VM] * 9,
        out_specs=(hbm, VM, VM, VM, VM),
        scratch_shapes=[
            tile, tile,
            pltpu.VMEM((2, 1, 16, 64, 512), BF),
            table, table,
            pltpu.VMEM((8192, 128), F32),
            blocks, blocks, blocks, blocks, blocks, blocks,
            image, image, near, near,
            pltpu.VMEM((3, 2, 64, 512), F32),
            pieces, pieces,
            pltpu.VMEM((1440, 512), BF),
            pltpu.VMEM((1440, 512), BF),
            pltpu.VMEM((66 * 32, 512), BF),
            pltpu.VMEM((2048, 512), F32),
            pltpu.VMEM((256, 432), F32),
            pltpu.VMEM((256, 432), F32),
            pltpu.VMEM((256, 128), F32),
            pltpu.VMEM((16, 32, 128), F32),
            pltpu.VMEM((8, 32, 128), F32),
            pltpu.VMEM((2, 54, 32), F32),
            pltpu.VMEM((256, 128), F32),
            pltpu.VMEM((256, 432), BF),
            pltpu.VMEM((256, 432), BF),
            pltpu.VMEM((144, 320), BF),
            pltpu.VMEM((8, 54, 432), BF),
            pltpu.VMEM((8, 54, 432), BF),
            pltpu.VMEM((10, 54, 144), BF),
            pltpu.SemaphoreType.DMA((8,)),
            pltpu.SemaphoreType.DMA((12,)),
            pltpu.SemaphoreType.DMA((12,)),
            pltpu.SemaphoreType.DMA((4,)),
        ],
        compiler_params=pltpu.CompilerParams(
            collective_id=0, has_side_effects=True, vmem_limit_bytes=VMEM_LIMIT
        ),
        name="cascade",
    )(*operands)


def on_device(
    kspace, measured, sample_mask, step_size, coil_field, conv_in, bias_in, conv_out, cotangent
):
    count_y, count_z = lax.axis_size("gy"), lax.axis_size("gz")
    row_tile, x_cells, depth_tile = kspace.shape[3], kspace.shape[4], kspace.shape[2]
    inverse_y = jnp.asarray(inverse_y_table(count_y, row_tile))
    forward_y = jnp.asarray(forward_y_table(count_y, row_tile))
    inverse_z = jnp.asarray(z_table(count_z * depth_tile, True))
    forward_z = jnp.asarray(z_table(count_z * depth_tile, False))
    norm = 1.0 / math.sqrt(x_cells * row_tile * count_y * depth_tile * count_z)
    refine, weight, grad_in, grad_bias, grad_out = run_cascade(
        norm, kspace, cotangent, coil_field, inverse_y, forward_y,
        jnp.asarray(band_spread()), jnp.asarray(band_spread_flipped()), jnp.asarray(out_spread()),
        inverse_z, forward_z, sample_mask, step_size.reshape(1, 1),
        conv_in.transpose(2, 3, 4, 1, 0).reshape(27, 2, 32), bias_in.reshape(1, 32),
        conv_out.transpose(2, 3, 4, 0, 1).reshape(27, 2, 32),
        jnp.asarray(band_keep()), jnp.asarray(band_gather()),
    )
    current = kspace.astype(F32)
    kspace_next = current - weight * (current - measured.astype(F32)) + refine.astype(F32)
    kspace_next = kspace_next.astype(BF)
    grad_in = grad_in.reshape(3, 3, 3, 2, 32).transpose(4, 3, 0, 1, 2)
    grad_out = grad_out.reshape(3, 3, 3, 2, 32).transpose(3, 4, 0, 1, 2)
    return kspace_next, grad_in, grad_bias.reshape(32), grad_out


def solution(mesh):
    tile = P(None, None, "gz", "gy", None)
    in_specs = (
        tile,
        tile,
        P("gz", "gy"),
        P(),
        P(None, AXES, None, None, None),
        P(),
        P(),
        P(),
        tile,
    )
    out_specs = (tile, P(), P(), P())
    return jax.shard_map(
        on_device, mesh=mesh, in_specs=in_specs, out_specs=out_specs, check_vma=False
    )
```

```python
import functools
import math

import jax
import jax.numpy as jnp
import numpy as np
from jax import lax
from jax.experimental import pallas as pl
from jax.experimental.pallas import tpu as pltpu
from jax.sharding import PartitionSpec as P

MESH = pl.DeviceIdType.MESH
AXES = ("gy", "gz")
BF = jnp.bfloat16
F32 = jnp.float32
VMEM_LIMIT = 56 * 2**20
VM = pl.BlockSpec(memory_space=pltpu.VMEM)


def trig(length):
    index = np.arange(length, dtype=np.int64)
    angle = (index[:, None] * index[None, :] % length).astype(np.float64) * (2.0 * math.pi / length)
    factor = 1.0 / math.sqrt(length)
    return np.cos(angle) * factor, np.sin(angle) * factor


def as_bf16(array):
    return np.asarray(array, dtype=np.float32).astype(jnp.bfloat16)


def inverse_y_table(gy, rows):
    length = gy * rows
    cos, sin = trig(length)
    cos, sin = cos.reshape(gy, rows, length), sin.reshape(gy, rows, length)
    table = np.stack([np.stack([cos, sin], 2), np.stack([-sin, cos], 2)], 1)
    return as_bf16(table.reshape(2 * length, 2 * length))


def forward_y_table(gy, rows):
    length = gy * rows
    cos, sin = trig(length)
    cos, sin = cos.reshape(length, gy, rows), sin.reshape(length, gy, rows)
    table = np.stack([np.stack([cos, -sin], 2), np.stack([sin, cos], 2)], 0)
    return as_bf16(table.reshape(2 * length, 2 * length))


def z_table(length, inverse):
    cos, sin = trig(length)
    if inverse:
        table = np.block([[cos, -sin], [sin, cos]])
    else:
        table = np.block([[cos, sin], [-sin, cos]])
    return as_bf16(table)


def band_masks():
    zo, dz, j, zi = np.ogrid[0:8, 0:3, 0:3, 0:8]
    return (8 * (j - 1) + zi == zo + dz - 1).astype(np.float32)


def band_spread():
    hit = band_masks()
    eye = np.eye(18, dtype=np.float32)
    spread = np.einsum("odjz,kl->odkjlz", hit, eye)
    return as_bf16(spread.reshape(8, 54, 432))


def band_keep():
    hit = band_masks()
    keep = np.broadcast_to(hit.transpose(1, 0, 2, 3)[:, :, :, None, :], (3, 8, 3, 18, 8))
    return np.ascontiguousarray(keep.reshape(3, 8, 432)).astype(np.float32)


def band_spread_flipped():
    spread = band_spread().reshape(8, 3, 3, 3, 2, 432)
    return np.ascontiguousarray(spread[:, ::-1, ::-1, ::-1].reshape(8, 54, 432))


def band_gather():
    eye = np.eye(18, dtype=np.float32)
    both = np.stack([eye, eye.reshape(18, 3, 3, 2)[:, ::-1, ::-1].reshape(18, 18)])
    both = np.broadcast_to(both[:, None, :, None, :], (2, 3, 18, 8, 18))
    return np.ascontiguousarray(both.reshape(2, 432, 18))


def out_spread():
    q, dz, zo = np.ogrid[0:10, 0:3, 0:8]
    hit = (q == zo + dz).astype(np.float32)
    three, two = np.eye(3, dtype=np.float32), np.eye(2, dtype=np.float32)
    spread = np.einsum("qdz,yY,xX,oO->qdyxoXOYz", hit, three, three, two)
    return as_bf16(spread.reshape(10, 54, 144))


AHEAD = 24
ROWS = 4
COILS = 2
BESIDE = 16
AFTER_IMAGE = AHEAD + ROWS + 8 * COILS
CONV = 2
BACK = 4


def shifted(value, dy):
    if dy == 1:
        return value
    lane = lax.broadcasted_iota(jnp.int32, value.shape, value.ndim - 1)
    if dy == 0:
        return jnp.where(lane == 0, 0.0, pltpu.roll(value, 1, value.ndim - 1))
    return jnp.where(lane == 511, 0.0, pltpu.roll(value, 511, value.ndim - 1))


def clear_columns(cols):
    cols[pl.ds(0, 144), :] = jnp.zeros((144, 512), BF)
    cols[pl.ds(1296, 144), :] = jnp.zeros((144, 512), BF)


def fill_columns(dx, image, cols):
    parts = [image(i) for i in range(2)]
    for dy in range(3):
        pair = jnp.stack([shifted(part, dy).reshape(8, 8, 512) for part in parts], axis=1)
        pair = pair.reshape(8, 16, 512).astype(BF)
        for zb in range(8):
            cols[pl.ds((zb + 1) * 144 + (dy * 3 + dx) * 16, 16), :] = pair[zb]


def gather_terms(total, keep, gather, order):
    pieces = []
    total = total.reshape(8, 32, 432)
    for dz in order:
        kept = total[0] * keep[dz, 0:1, :]
        for zo in range(1, 8):
            kept = kept + total[zo] * keep[dz, zo : zo + 1, :]
        pieces.append(
            jnp.dot(kept, gather, preferred_element_type=F32, precision=lax.Precision.HIGHEST)
        )
    return pieces


def cascade(
    norm,
    k_hbm, g_hbm, s_hbm, iy_hbm, fy_hbm, spread_in_hbm, spread_back_hbm, spread_out_hbm,
    iz, fz, mask, step, taps_in, bias, taps_out, keep, gather,
    out_hbm, weight, grad_in, grad_bias, grad_out,
    kv, gv, sens, iy, fy, stage, sk, sg, sf, rk, rg, rf,
    own_k, own_g, near_k, near_g, q_mid, q_send, q_near,
    cols, cols_g, hidden, slope, sum_in, sum_out, sum_b, first, second,
    flat, bias_cols, w_in, w_back, w_out, spread_in, spread_back, spread_out,
    load_sem, send_sem, recv_sem, store_sem,
):
    my_y, my_z = lax.axis_index("gy"), lax.axis_index("gz")
    me = my_y * 16 + my_z
    pos_x, pos_y, pos_z, pos_c = my_y % 4, my_y // 4 * 2 + my_z // 8, my_z // 2 % 4, my_z % 2
    left, right = (me + 127) % 128, (me + 1) % 128

    def pair(t):
        return (lax.div(t, 16), lax.rem(t, 16))

    loads = [
        pltpu.make_async_copy(src, dst, load_sem.at[n])
        for n, (src, dst) in enumerate(
            [(k_hbm, kv), (g_hbm, gv), (iy_hbm, iy), (s_hbm, sens), (fy_hbm, fy),
             (spread_in_hbm, spread_in), (spread_back_hbm, spread_back), (spread_out_hbm, spread_out)]
        )
    ]
    for load in loads:
        load.start()
    barrier = pltpu.get_barrier_semaphore()

    def greet(n, carry):
        pl.semaphore_signal(barrier, inc=1, device_id=pair(lax.rem(me + n, 128)), device_id_type=MESH)
        return carry

    lax.fori_loop(1, 128, greet, 0, unroll=4)

    def remote(src, dst, n, t):
        return pltpu.make_async_remote_copy(
            src_ref=src,
            dst_ref=dst,
            send_sem=send_sem.at[n],
            recv_sem=recv_sem.at[n],
            device_id=pair(t),
            device_id_type=MESH,
        )

    def target(i):
        n = lax.rem(i * 45, 128)
        x = lax.rem(pos_x + lax.rem(lax.div(n, 2), 4), 4)
        y = lax.rem(pos_y + lax.rem(lax.div(n, 8), 4), 4)
        z = lax.rem(pos_z + lax.div(n, 32), 4)
        c = lax.rem(pos_c + lax.rem(n, 2), 2)
        return (lax.div(y, 2) * 4 + x) * 16 + lax.rem(y, 2) * 8 + z * 2 + c

    nt = (((1,), (1,)), ((), ()))

    def turn(source, index):
        depth, coil = index // 16, index % 16
        both = jnp.concatenate([source[0, coil, depth], source[1, coil, depth]], axis=0)
        stage[pl.ds(index, 128, stride=64), :] = both.T.astype(F32)

    def block_of(t):
        return stage[pl.ds(pl.multiple_of(t * 64, 64), 64), :].astype(BF)

    def turn_k(index, carry):
        turn(kv, index)
        return carry

    def half_of(t, half):
        return stage[pl.ds(pl.multiple_of(t * 64 + half * 32, 32), 32), :].astype(BF)

    loads[0].wait()
    for half in range(2):
        rows = pl.ds(half * 32, 32)

        def send_k(i, carry):
            t = target(i)
            sk[t, rows] = half_of(t, half)
            remote(sk.at[t, rows], rk.at[me, rows], 11 * half, t).start()
            return carry

        lax.fori_loop(half * 32, half * 32 + 32, turn_k, 0, unroll=4)
        if half == 0:
            pl.semaphore_wait(barrier, 127)
        rk[me, rows] = half_of(me, half)
        lax.fori_loop(1, 128, send_k, 0, unroll=2)

    def turn_g(index, carry):
        turn(gv, index)
        return carry

    def keep_g(i, carry):
        sg[i] = block_of(i)
        return carry

    def later_g(i, carry):
        t = target(i)
        remote(sg.at[t], rg.at[me], 1, t).start()
        return carry

    loads[1].wait()
    lax.fori_loop(0, 64, turn_g, 0, unroll=4)
    rg[me] = block_of(me)
    lax.fori_loop(0, 128, keep_g, 0, unroll=4)
    lax.fori_loop(1, AHEAD, later_g, 0)

    for n in (5, 6, 7):
        loads[n].wait()
    contract = (((0,), (0,)), ((), ()))
    for tap in range(27):
        flat[0, pl.ds(tap * 2, 2), :] = taps_in[tap].astype(F32)
        flat[1, pl.ds(tap * 2, 2), :] = taps_out[tap].astype(F32)
    flat_in, flat_out = flat[0].astype(BF), flat[1].astype(BF)
    for zo in range(8):
        rows = pl.ds(zo * 32, 32)
        band = lax.dot_general(flat_in, spread_in[zo], contract, preferred_element_type=F32)
        w_in[rows, :] = band.astype(BF)
        band = lax.dot_general(flat_out, spread_back[zo], contract, preferred_element_type=F32)
        w_back[rows, :] = band.astype(BF)
    bands = [
        lax.dot_general(spread_out[q], flat_out, contract, preferred_element_type=F32)
        for q in range(10)
    ]
    w_out[...] = jnp.concatenate(bands, axis=1).astype(BF)

    def upright(row):
        return jnp.broadcast_to(row, (128, 128)).T

    bias_rows = upright(jnp.concatenate([bias[...]] * 4, axis=1))[:32]
    for zo in range(8):
        bias_cols[pl.ds(zo * 32, 32), :] = bias_rows
    for depth in range(4):
        row = mask[pl.ds(depth, 1), :].astype(F32) * step[...]
        weight[depth] = upright(jnp.concatenate([row, row], axis=1))[:64]

    def wait_blocks(sent, got, n, rows=64):
        every = pltpu.make_async_remote_copy(
            src_ref=sent.at[pl.ds(0, 127), pl.ds(0, rows)],
            dst_ref=got.at[pl.ds(0, 127), pl.ds(0, rows)],
            send_sem=send_sem.at[n],
            recv_sem=recv_sem.at[n],
            device_id=pair(right),
            device_id_type=MESH,
        )
        every.wait_send()
        every.wait_recv()

    def both_ways(up, down, near, n):
        return [remote(up, near.at[0], n, right), remote(down, near.at[1], n + 1, left)]

    def to_image(tiles, image, near, n, push, *arrivals):
        parts = len(arrivals)
        depth = 64 // parts

        for part, (sent, sem) in enumerate(arrivals):
            wait_blocks(sent, tiles, sem, depth)

            def rows(m, carry):
                push(AHEAD + 4 // parts * part + m, 0)
                lines = jnp.concatenate(
                    [
                        tiles[pl.ds(gy * 16 + m * 4 * parts, 4 * parts), pl.ds(part * depth, depth)]
                        .reshape(256, 128)
                        for gy in range(8)
                    ],
                    axis=1,
                )
                done = jnp.dot(lines, iy[...], preferred_element_type=F32)
                done = done.reshape(4 * parts, depth, 1024)
                for lt in range(8):
                    for k in range(4 * parts):
                        start = lt * 1024 + (m * 4 * parts + k) * 64 + part * depth
                        stage[pl.ds(pl.multiple_of(start, 32), depth), :] = done[
                            k, :, lt * 128 : lt * 128 + 128
                        ]
                return carry

            lax.fori_loop(0, 4 // parts, rows, 0)

        for chunk in range(4):
            lane = pl.ds(chunk * 128, 128)

            def coils(step_c, carry):
                real, imag = carry
                if chunk < COILS:
                    push(AHEAD + ROWS + chunk * 8 + step_c, 0)
                lines = []
                for c in (2 * step_c, 2 * step_c + 1):
                    halves = [
                        stage[pl.ds((p * 4 + chunk) * 1024 + c, 64, stride=16), :] for p in range(2)
                    ]
                    lines.append(jnp.concatenate(halves, axis=0).astype(BF))
                done = jnp.dot(
                    iz[...], jnp.concatenate(lines, axis=1), preferred_element_type=F32
                )
                for k in range(2):
                    c = 2 * step_c + k
                    c_r, c_i = done[:64, k * 128 : k * 128 + 128], done[64:, k * 128 : k * 128 + 128]
                    s_r, s_i = sens[0, 0, c, :, lane].astype(F32), sens[1, 0, c, :, lane].astype(F32)
                    real = real + (s_r * c_r + s_i * c_i)
                    imag = imag + (s_r * c_i - s_i * c_r)
                return real, imag

            zero = jnp.zeros((64, 128), F32)
            real, imag = lax.fori_loop(0, 8, coils, (zero, zero), unroll=4)
            image[chunk, 0] = real.astype(BF)
            image[chunk, 1] = imag.astype(BF)
            remote(image.at[chunk], near.at[0, chunk], n, right).start()
            remote(image.at[chunk], near.at[1, chunk], n + 1, left).start()
        return both_ways(image, image, near, n)

    def inside(side, value):
        return jnp.where(me > 0 if side == 0 else me < 127, value, 0.0)

    def plane(image, i):
        return jnp.concatenate([image[chunk, i] for chunk in range(4)], axis=1).astype(F32)

    def fill(own, near, copies, columns):
        fill_columns(1, lambda i: plane(own, i), columns)
        for side, copy in enumerate(copies):
            copy.wait()
            fill_columns(2 * side, lambda i: inside(side, plane(near.at[side], i)), columns)

    loads[2].wait()
    loads[3].wait()
    copies = to_image(rk, own_k, near_k, 3, later_g, (sk, 0), (sk, 11))
    lax.fori_loop(AFTER_IMAGE, AFTER_IMAGE + BESIDE, later_g, 0)
    clear_columns(cols)
    fill(own_k, near_k, copies, cols)
    hidden[pl.ds(0, 32), :] = jnp.zeros((32, 512), BF)
    hidden[pl.ds(65 * 32, 32), :] = jnp.zeros((32, 512), BF)

    def conv_in_block(zb, carry):
        for i in range(CONV):
            later_g(AFTER_IMAGE + BESIDE + zb * CONV + i, 0)
        window = cols[pl.ds(pl.multiple_of(zb * 144, 16), 432), :]
        pre = jnp.dot(w_in[...], window, preferred_element_type=F32)
        pre = pre + jnp.concatenate([bias_cols[...]] * 4, axis=1)
        sig = jax.nn.sigmoid(pre)
        hidden[pl.ds(pl.multiple_of(zb * 256 + 32, 32), 256), :] = (pre * sig).astype(BF)
        slope[pl.ds(pl.multiple_of(zb * 256, 256), 256), :] = sig * (1.0 + pre * (1.0 - sig))
        return carry

    lax.fori_loop(0, 8, conv_in_block, 0, unroll=2)

    def conv_out_block(zb, carry):
        for i in range(CONV):
            later_g(AFTER_IMAGE + BESIDE + 8 * CONV + zb * CONV + i, 0)
        window = hidden[pl.ds(pl.multiple_of(zb * 256, 256), 320), :]
        terms = jnp.dot(w_out[...], window, preferred_element_type=F32).reshape(18, 8, 512)
        rows = pl.ds(pl.multiple_of(zb * 8, 8), 8)
        for dx in range(3):
            for o in range(2):
                base = (dx * 2 + o) * 3
                total = shifted(terms[base], 0) + terms[base + 1] + shifted(terms[base + 2], 2)
                q_mid[dx, o, rows, :] = total
        return carry

    for piece in range(4):
        lax.fori_loop(piece * 2, piece * 2 + 2, conv_out_block, 0, unroll=2)
        rows = pl.ds(piece * 16, 16)
        q_send[0, piece] = q_mid[0, :, rows, :].astype(BF)
        q_send[1, piece] = q_mid[2, :, rows, :].astype(BF)
        remote(q_send.at[0, piece], q_near.at[0, piece], 5, right).start()
        remote(q_send.at[1, piece], q_near.at[1, piece], 6, left).start()
    lax.fori_loop(AFTER_IMAGE + BESIDE + 16 * CONV, 128, later_g, 0)
    for copy in both_ways(q_send.at[0], q_send.at[1], q_near, 5):
        copy.wait()

    for piece in range(4):
        rows = pl.ds(piece * 16, 16)
        for o in range(2):
            total = inside(0, q_near[0, piece, o].astype(F32)) + q_mid[1, o, rows, :]
            total = total + inside(1, q_near[1, piece, o].astype(F32))
            q_mid[0, o, rows, :] = total.astype(BF).astype(F32)
    for chunk in range(4):
        lane = pl.ds(chunk * 128, 128)
        r_r, r_i = q_mid[0, 0, :, lane], q_mid[0, 1, :, lane]

        def spread(step_c, carry):
            lines = []
            for c in (2 * step_c, 2 * step_c + 1):
                s_r, s_i = sens[0, 0, c, :, lane].astype(F32), sens[1, 0, c, :, lane].astype(F32)
                both = [s_r * r_r - s_i * r_i, s_r * r_i + s_i * r_r]
                lines.append(jnp.concatenate(both, axis=0).astype(BF))
            done = jnp.dot(fz[...], jnp.concatenate(lines, axis=1), preferred_element_type=F32)
            for k in range(2):
                for p in range(2):
                    rows = pl.ds((p * 4 + chunk) * 1024 + 2 * step_c + k, 64, stride=16)
                    stage[rows, :] = done[p * 64 : p * 64 + 64, k * 128 : k * 128 + 128]
            return carry

        lax.fori_loop(0, 8, spread, 0, unroll=4)
    loads[4].wait()

    def send_f(m, carry):
        lines = [stage[pl.ds(pl.multiple_of(lt * 1024 + m * 256, 256), 256), :] for lt in range(8)]
        lines = jnp.concatenate([part.astype(BF) for part in lines], axis=1)
        done = jnp.dot(lines, fy[...], preferred_element_type=F32).astype(BF)
        for gy in range(8):
            sf[pl.ds(gy * 16 + m * 4, 4)] = done[:, gy * 128 : gy * 128 + 128].reshape(4, 64, 128)

        return carry

    def start_f(i, carry):
        t = target(i)
        remote(sf.at[t], rf.at[me], 2, t).start()
        return carry

    lax.fori_loop(0, 4, send_f, 0, unroll=2)
    rf[me] = sf[me]
    lax.fori_loop(1, AHEAD, start_f, 0)

    copies = to_image(rg, own_g, near_g, 7, start_f, (sg, 1))
    lax.fori_loop(AFTER_IMAGE, AFTER_IMAGE + BESIDE, start_f, 0)
    clear_columns(cols_g)
    fill(own_g, near_g, copies, cols_g)
    sum_in[...] = jnp.zeros_like(sum_in)
    sum_out[...] = jnp.zeros_like(sum_out)
    sum_b[...] = jnp.zeros_like(sum_b)
    def back_block(zb, carry):
        for i in range(BACK):
            start_f(AFTER_IMAGE + BESIDE + zb * BACK + i, 0)
        span = pl.ds(pl.multiple_of(zb * 144, 16), 432)
        window_g = cols_g[span, :]
        back = jnp.dot(w_back[...], window_g, preferred_element_type=F32)
        back = (back * slope[pl.ds(pl.multiple_of(zb * 256, 256), 256), :]).astype(BF)
        sum_in[...] += lax.dot_general(back, cols[span, :], nt, preferred_element_type=F32)
        held = hidden[pl.ds(pl.multiple_of(zb * 256 + 32, 32), 256), :]
        sum_out[...] += lax.dot_general(held, window_g, nt, preferred_element_type=F32)
        wide = back.astype(F32)
        sum_b[...] += wide[:, :128] + wide[:, 128:256] + wide[:, 256:384] + wide[:, 384:]
        return carry

    lax.fori_loop(0, 8, back_block, 0, unroll=2)
    lax.fori_loop(AFTER_IMAGE + BESIDE + 8 * BACK, 128, start_f, 0)
    bias_sum = jnp.sum(sum_b[...].reshape(8, 32, 128), axis=0)
    bias_sum = jnp.sum(bias_sum, axis=1, keepdims=True)
    pieces = gather_terms(sum_in[...], keep, gather[0], (0, 1, 2))
    pieces += gather_terms(sum_out[...], keep, gather[1], (2, 1, 0))
    pieces.append(jnp.broadcast_to(bias_sum, (32, 20)))

    def share(buffer, mine, count, n, device):
        def start(step, carry):
            remote(buffer.at[mine], buffer.at[mine], n, device((mine + step) % count)).start()
            return carry

        lax.fori_loop(1, count, start, 0)

    def collect(buffer, count, n):
        every = pltpu.make_async_remote_copy(
            src_ref=buffer.at[pl.ds(0, count - 1)],
            dst_ref=buffer.at[pl.ds(0, count - 1)],
            send_sem=send_sem.at[n],
            recv_sem=recv_sem.at[n],
            device_id=pair(right),
            device_id_type=MESH,
        )
        every.wait_send()
        every.wait_recv()
        total = buffer[0]
        for index in range(1, count):
            total = total + buffer[index]
        return total

    first[my_z] = jnp.concatenate(pieces, axis=1)
    share(first, my_z, 16, 9, lambda to: my_y * 16 + to)

    wait_blocks(sf, rf, 2)

    second[my_y] = collect(first, 16, 9)
    share(second, my_y, 8, 10, lambda to: to * 16 + my_z)

    def widen(x, carry):
        stage[pl.ds(pl.multiple_of(x * 64, 64), 64), :] = rf[x].astype(F32)
        return carry

    lax.fori_loop(0, 128, widen, 0, unroll=8)
    def finish(index, carry):
        depth, coil = lax.div(index, 16), lax.rem(index, 16)
        both = stage[pl.ds(index, 128, stride=64), :].astype(BF).T
        kv[0, coil, depth], kv[1, coil, depth] = both[:64], both[64:]
        return carry

    stores = []
    for depth in range(4):
        lax.fori_loop(depth * 16, depth * 16 + 16, finish, 0, unroll=4)
        stores.append(
            pltpu.make_async_copy(kv.at[:, :, depth], out_hbm.at[:, :, depth], store_sem.at[depth])
        )
        stores[-1].start()
    total = jnp.concatenate([collect(second, 8, 10) * norm] * 4, axis=0).T[:, :32]
    for tap in range(27):
        grad_in[tap] = total[tap * 2 : tap * 2 + 2]
        grad_out[tap] = total[54 + tap * 2 : 56 + tap * 2]
    grad_bias[...] = total[108:109]
    for store in stores:
        store.wait()


def run_cascade(norm, *operands):
    blocks = pltpu.VMEM((128, 64, 128), BF)
    tile = pltpu.VMEM((2, 16, 4, 64, 128), BF)
    image = pltpu.VMEM((4, 2, 64, 128), BF)
    near = pltpu.VMEM((2, 4, 2, 64, 128), BF)
    pieces = pltpu.VMEM((2, 4, 2, 16, 512), BF)
    table = pltpu.VMEM((1024, 1024), BF)
    hbm = pl.BlockSpec(memory_space=pl.ANY)
    return pl.pallas_call(
        functools.partial(cascade, norm),
        out_shape=(
            jax.ShapeDtypeStruct((2, 16, 4, 64, 128), BF),
            jax.ShapeDtypeStruct((4, 64, 128), F32),
            jax.ShapeDtypeStruct((27, 2, 32), F32),
            jax.ShapeDtypeStruct((1, 32), F32),
            jax.ShapeDtypeStruct((27, 2, 32), F32),
        ),
        in_specs=[hbm] * 8 + [VM] * 9,
        out_specs=(hbm, VM, VM, VM, VM),
        scratch_shapes=[
            tile, tile,
            pltpu.VMEM((2, 1, 16, 64, 512), BF),
            table, table,
            pltpu.VMEM((8192, 128), F32),
            blocks, blocks, blocks, blocks, blocks, blocks,
            image, image, near, near,
            pltpu.VMEM((3, 2, 64, 512), F32),
            pieces, pieces,
            pltpu.VMEM((1440, 512), BF),
            pltpu.VMEM((1440, 512), BF),
            pltpu.VMEM((66 * 32, 512), BF),
            pltpu.VMEM((2048, 512), F32),
            pltpu.VMEM((256, 432), F32),
            pltpu.VMEM((256, 432), F32),
            pltpu.VMEM((256, 128), F32),
            pltpu.VMEM((16, 32, 128), F32),
            pltpu.VMEM((8, 32, 128), F32),
            pltpu.VMEM((2, 54, 32), F32),
            pltpu.VMEM((256, 128), F32),
            pltpu.VMEM((256, 432), BF),
            pltpu.VMEM((256, 432), BF),
            pltpu.VMEM((144, 320), BF),
            pltpu.VMEM((8, 54, 432), BF),
            pltpu.VMEM((8, 54, 432), BF),
            pltpu.VMEM((10, 54, 144), BF),
            pltpu.SemaphoreType.DMA((8,)),
            pltpu.SemaphoreType.DMA((12,)),
            pltpu.SemaphoreType.DMA((12,)),
            pltpu.SemaphoreType.DMA((4,)),
        ],
        compiler_params=pltpu.CompilerParams(
            collective_id=0, has_side_effects=True, vmem_limit_bytes=VMEM_LIMIT
        ),
        name="cascade",
    )(*operands)


def on_device(
    kspace, measured, sample_mask, step_size, coil_field, conv_in, bias_in, conv_out, cotangent
):
    count_y, count_z = lax.axis_size("gy"), lax.axis_size("gz")
    row_tile, x_cells, depth_tile = kspace.shape[3], kspace.shape[4], kspace.shape[2]
    inverse_y = jnp.asarray(inverse_y_table(count_y, row_tile))
    forward_y = jnp.asarray(forward_y_table(count_y, row_tile))
    inverse_z = jnp.asarray(z_table(count_z * depth_tile, True))
    forward_z = jnp.asarray(z_table(count_z * depth_tile, False))
    norm = 1.0 / math.sqrt(x_cells * row_tile * count_y * depth_tile * count_z)
    refine, weight, grad_in, grad_bias, grad_out = run_cascade(
        norm, kspace, cotangent, coil_field, inverse_y, forward_y,
        jnp.asarray(band_spread()), jnp.asarray(band_spread_flipped()), jnp.asarray(out_spread()),
        inverse_z, forward_z, sample_mask, step_size.reshape(1, 1),
        conv_in.transpose(2, 3, 4, 1, 0).reshape(27, 2, 32), bias_in.reshape(1, 32),
        conv_out.transpose(2, 3, 4, 0, 1).reshape(27, 2, 32),
        jnp.asarray(band_keep()), jnp.asarray(band_gather()),
    )
    current = kspace.astype(F32)
    kspace_next = current - weight * (current - measured.astype(F32)) + refine.astype(F32)
    kspace_next = kspace_next.astype(BF)
    grad_in = grad_in.reshape(3, 3, 3, 2, 32).transpose(4, 3, 0, 1, 2)
    grad_out = grad_out.reshape(3, 3, 3, 2, 32).transpose(3, 4, 0, 1, 2)
    return kspace_next, grad_in, grad_bias.reshape(32), grad_out


def solution(mesh):
    tile = P(None, None, "gz", "gy", None)
    in_specs = (
        tile,
        tile,
        P("gz", "gy"),
        P(),
        P(None, AXES, None, None, None),
        P(),
        P(),
        P(),
        tile,
    )
    out_specs = (tile, P(), P(), P())
    return jax.shard_map(
        on_device, mesh=mesh, in_specs=in_specs, out_specs=out_specs, check_vma=False
    )
```
